1024 devices in a mesh: expert: 32 (over z, core), dp: 32 (over y, x).
Axes of the slice: x: 4, y: 8, z: 16, core: 2. Of those that a mesh axis runs over, the one named last changes fastest.
Arguments:
- out_grad: bfloat16 [32, 512, 2048], P('dp', 'expert'), may hold values from -200 to 200
- routes: int32 [32, 512, 8], P('dp', 'expert'), may hold values from 0 to 31, all different within a row; in each aligned block of 16 rows (0 to 15, 16 to 31, ..., all dimensions but the last counted through in order) at most 5 rows name the same one
- gate_probs: float32 [32, 512, 8], P('dp', 'expert'), may hold values from 0.1 to 0.6
- hidden: bfloat16 [32, 32, 160, 768], P('dp', 'expert'), may hold values from -60 to 60
- first_prev: float32 [32, 768, 2048], P('expert', 'dp'), may hold values from -0.125 to 0.125
- second_prev: float32 [32, 768, 2048], P('expert', 'dp'), may hold values from 1.2207031e-05 to 0.00012207031
Outputs:
- update: float32 [32, 768, 2048], P('expert', 'dp')
- lr_scale: float32 [32], P('expert')
The draws below stay inside these ranges and needn't reach their ends.
Inputs may be any that keep to these rules, and one draw needn't show every extreme that they name: `routes`: each token names 8 different experts; among the 16 tokens of one device no expert is named more than 5 times.
All inputs are finite; a program needn't handle non-finite values.
Results may differ from the reference program's by a relative error of at most 0.0055.
Values may be sent and summed in bfloat16 or wider, within the bound.
A program may use at most 64 MiB of HBM per device.

```python
import math
import jax
import jax.numpy as jnp
import numpy as np
from jax import lax

D = 2048
FW = 768
TOP = 8
TOK_DEV = 16
PAD = 16
ADAM_STEP = 3
EXPERTS = 32
CAP = 5
SLOTS = 160
TOKENS = 512
N_EXPERT = 32
N_DP = 32


def replica_factor(exponent):
    steps_along = jnp.arange(N_DP, dtype=jnp.float32) / max(N_DP - 1, 1)
    return jnp.exp(exponent * jnp.log(3.0) * steps_along)


def draw_out_grad(key, part):
    key = jax.random.fold_in(key, 11)
    key_base = jax.random.fold_in(key, 0)
    key_rows = jax.random.fold_in(key, 1)
    key_cols = jax.random.fold_in(key, 2)
    key_pattern = jax.random.fold_in(key, 4)
    row_scale = jnp.exp(jax.random.uniform(key_rows, (N_DP, TOKENS, 1)) * jnp.log(10.0)) / 4.0
    col_scale = jnp.exp(jax.random.uniform(key_cols, (1, 1, D)) * jnp.log(10.0)) / 4.0
    col_pattern = jnp.clip(jax.random.normal(key_pattern, (1, 1, D)), -3.0, 3.0)
    base_values = jax.random.normal(key_base, (N_DP, TOKENS, D))
    factor = replica_factor(0.5)
    return ((base_values + col_pattern) * row_scale * col_scale * factor[:, None, None]).astype(jnp.bfloat16)


def draw_hidden(key, part):
    key = jax.random.fold_in(key, 23)
    key_base, key_rows, key_cols, key_pattern, key_share = jax.random.split(key, 5)
    row_scale = jnp.exp(jax.random.uniform(key_rows, (N_DP, EXPERTS, SLOTS, 1)) * jnp.log(10.0)) / 4.0
    col_scale = jnp.exp(jax.random.uniform(key_cols, (1, 1, 1, FW)) * jnp.log(10.0)) / 4.0
    col_pattern = jnp.clip(jax.random.normal(key_pattern, (1, 1, 1, FW)), -3.0, 3.0)
    ranks = jax.random.permutation(key_share, EXPERTS).astype(jnp.float32)
    share = ((ranks + 0.5) / EXPERTS * 8.0 / (TOK_DEV * TOP) ** 0.5).reshape(1, EXPERTS, 1, 1)
    base_values = jax.random.normal(key_base, (N_DP, EXPERTS, SLOTS, FW))
    return ((base_values + share * col_pattern) * row_scale * col_scale).astype(jnp.bfloat16)


def steps_of(own_key, shape, shards, low, high):
    gain, own = 1.0, jax.random.fold_in(own_key, 6)
    for axis_at, shards_of in shards:
        heights = jnp.exp(jax.random.uniform(jax.random.fold_in(own, axis_at), (shards_of,), jnp.float32, low / len(shards), high / len(shards)))
        gain = gain * jnp.repeat(heights, shape[axis_at] // shards_of).reshape([-1 if axis == axis_at else 1 for axis in range(len(shape))])
    return gain


def deal_out(key, own, number, rows, number_of, top, limit, lean):
    order = jax.random.permutation(key, number_of)
    heavy_load, ordinary = shares(number_of, rows * top, limit, lean, True), shares(number_of, rows * top, limit, lean, False)
    places = jnp.arange(number_of)

    def named(sizes, rotation):
        used = int((sizes > 0).sum())
        fixed = max(1, used // 4)
        shifted = fixed + (places - fixed + rotation * (used - fixed)) % max(1, number_of - fixed)
        return jnp.zeros((number_of,), jnp.int32).at[order[jnp.where(places < fixed, places, shifted)]].set(jnp.asarray(sizes, jnp.int32))

    sizes = jnp.where(number % 4 == 0, named(heavy_load, number // 4), named(ordinary, number - number // 4 - 1))
    mixed = jax.random.permutation(jax.random.fold_in(own, 3), number_of)
    donor, receiver = mixed[0:number_of // 2 * 2:2], mixed[1:number_of // 2 * 2:2]
    slack = jnp.minimum(sizes[donor] - 1, limit - sizes[receiver]) // 2
    slack = jnp.where((donor == order[0]) | (receiver == order[0]) | (sizes[receiver] == 0), 0, jnp.maximum(slack, 0))
    shifted = jax.random.randint(jax.random.fold_in(own, 4), (number_of // 2,), 0, 1 << 20) % (slack + 1)
    sizes = sizes.at[donor].add(-shifted).at[receiver].add(shifted)
    labels = jnp.searchsorted(jnp.cumsum(sizes), jnp.arange(rows * top), side="right").astype(jnp.int32)
    table = labels.reshape(top, rows).T
    table = table[jax.random.permutation(jax.random.fold_in(own, 1), rows)]
    rotation = jax.random.randint(jax.random.fold_in(own, 2), (rows, 1), 0, top)
    return jnp.take_along_axis(table, (jnp.arange(top)[None, :] + rotation) % top, axis=1)


def shares(amount, total, most, lean, full):
    loads = [(1 << 20) // math.isqrt(standing ** lean) + 1 for standing in range(1, amount + 1)]
    largest = most if full else min(most, max(-(-total // amount), total * loads[0] // sum(loads)))
    least = 1 if total - largest >= amount - 1 else 0
    counts, rest = [largest] + [least] * (amount - 1), total - largest - least * (amount - 1)
    while rest > 0:
        movable = [i for i in range(1, amount) if counts[i] < largest] or [i for i in range(1, amount) if counts[i] < most]
        pool, left = sum([loads[i] for i in movable]), rest
        for i in movable:
            addition = min(most - counts[i], max(1, left * loads[i] // pool), rest)
            counts[i] = counts[i] + addition
            rest = rest - addition
    return np.array(counts)


def normal_values(own_key, extent, spread, most, cuts=(), kind=jnp.bfloat16):
    array = spread * jax.random.normal(own_key, extent, jnp.float32)
    if cuts:
        array = array * steps_of(own_key, extent, cuts, -0.22, 0.18)
    return jnp.clip(array, -most, most).astype(kind)


def setup_inputs(seed: int = 0) -> dict:
    key_of = jax.random.split(jax.random.key(seed), 7)
    out_grad = draw_out_grad(jax.random.fold_in(key_of[6], 71), 0)
    routes_keys = jax.random.split(jax.random.fold_in(key_of[1], 1), N_DP * TOKENS // TOK_DEV)
    routes_turns = jax.random.permutation(jax.random.fold_in(key_of[1], 3), N_DP * TOKENS // TOK_DEV)
    routes = jax.vmap(lambda own, number: deal_out(jax.random.fold_in(key_of[1], 2), own, number, TOK_DEV, EXPERTS, TOP, CAP, 1))(routes_keys, routes_turns).reshape((N_DP, TOKENS, TOP))
    gate_probs = jnp.clip(0.1 + 0.5 * jax.random.uniform(key_of[2], (N_DP, TOKENS, TOP), jnp.float32) ** steps_of(key_of[2], (N_DP, TOKENS, TOP), ((0, 32), (1, 32)), -0.2, 0.2), 0.1, 0.6)
    hidden = draw_hidden(jax.random.fold_in(key_of[6], 71), 0)
    first_prev = normal_values(key_of[4], (EXPERTS, FW, D), (0.5 / (TOK_DEV * TOP * N_DP) ** 0.5), 0.125, ((0, 32), (1, 32)), jnp.float32)
    second_prev = jnp.clip(jnp.exp(math.log(0.00012207031) - 2.3025851 * jax.random.uniform(key_of[5], (EXPERTS, FW, D), jnp.float32) ** steps_of(key_of[5], (EXPERTS, FW, D), ((0, 32), (1, 32)), -0.2, 0.2)), 1.220703143189894e-05, 0.00012207031)
    return dict(out_grad=out_grad, routes=routes, gate_probs=gate_probs, hidden=hidden, first_prev=first_prev, second_prev=second_prev)


def dispatch_rows(tokens_here, chosen, weights_here, experts_all, capacity):
    onehot = (chosen[:, :, None] == jnp.arange(experts_all, dtype=jnp.int32)[None, None, :]).astype(jnp.float32)
    marked = lax.optimization_barrier(jnp.sum(onehot, axis=1))
    earlier = jnp.cumsum(marked, axis=0) - marked
    scaled = lax.optimization_barrier(jnp.sum(onehot * weights_here[:, :, None], axis=1))
    slot_ids = jnp.arange(capacity, dtype=jnp.float32)
    placing = scaled.T[:, None, :] * (earlier.T[:, None, :] == slot_ids[None, :, None]).astype(jnp.float32)
    outgoing = jnp.einsum('ect,td->ecd', placing, tokens_here.astype(jnp.float32), precision=lax.Precision.HIGHEST).astype(jnp.bfloat16)
    return (outgoing, lax.optimization_barrier(jnp.sum(marked, axis=0)))

def reference(out_grad, routes, gate_probs, hidden, first_prev, second_prev):

    def replica_step(running, inputs_here):
        grad_sum, spread_sum, total_rows = running
        grads_here, routes_here, probs_here, saved_here = inputs_here
        outgoing, counted = jax.vmap(lambda tok_block, route_block, prob_block: dispatch_rows(tok_block, route_block, prob_block, EXPERTS, CAP))(grads_here.reshape(N_EXPERT, TOK_DEV, D), routes_here.reshape(N_EXPERT, TOK_DEV, TOP), probs_here.reshape(N_EXPERT, TOK_DEV, TOP))
        received = jnp.swapaxes(outgoing, 0, 1).reshape(EXPERTS, SLOTS, D)

        def per_expert(pair):
            saved_one, rows_one = pair
            partial_one = jnp.dot(saved_one.T, rows_one, preferred_element_type=jnp.float32)
            return (partial_one.astype(jnp.bfloat16), jnp.sum(partial_one * partial_one))
        rounded, squares = lax.map(per_expert, (saved_here, received))
        routed = lax.optimization_barrier(jnp.sum(counted, axis=0)).astype(jnp.int32)
        padded = (routed + PAD - 1) // PAD * PAD
        grad_sum = grad_sum + lax.optimization_barrier(rounded).astype(jnp.float32)
        return ((grad_sum, spread_sum + squares, total_rows + padded.astype(jnp.float32)), None)
    start_state = (jnp.zeros((EXPERTS, FW, D), jnp.float32), jnp.zeros((EXPERTS,), jnp.float32), jnp.zeros((EXPERTS,), jnp.float32))
    (gradient, spread_sum, total_rows), unused = lax.scan(replica_step, start_state, (out_grad, routes, gate_probs, hidden))
    power_sum = lax.optimization_barrier(jnp.sum(gradient * gradient, axis=(1, 2)))
    noise_scale = total_rows * spread_sum / (N_DP * power_sum + 1e-06)
    lr_scale = noise_scale / (noise_scale + total_rows / N_DP)
    mean_grad = gradient / total_rows[:, None, None]
    first_moment = 0.9 * first_prev + 0.1 * mean_grad
    second_moment = 0.95 * second_prev + 0.05 * mean_grad * mean_grad
    update = -lr_scale[:, None, None] * (first_moment / (1.0 - 0.9 ** ADAM_STEP)) / (jnp.sqrt(second_moment / (1.0 - 0.95 ** ADAM_STEP)) + 1e-08)
    return (update, lr_scale)
```

```python
import functools

import jax
import jax.numpy as jnp
from jax import lax
from jax.experimental import pallas as pl
from jax.experimental.pallas import tpu as pltpu
from jax.sharding import PartitionSpec as P

PAD = 16
ADAM_STEP = 3
MESH = pl.DeviceIdType.MESH
NX, NY, NZ = 4, 8, 16
HIGHEST = lax.Precision.HIGHEST
F32 = jnp.float32
BF16 = jnp.bfloat16


def iota(shape, dim):
    return lax.broadcasted_iota(jnp.int32, shape, dim)


def kernel(
    grads, routes, gates, hidden, first_prev, second_prev,
    out, lr_out,
    tok, info, info_x, hid, hid_t, sent, part, send_y, recv_y, own, relay, vec_x, vec_y, mom1, mom2,
    sem_local, sem_tok_x, sem_info_x, sem_hid, sem_send_x,
    sem_z, sem_z_info, sem_sib, sem_sib_info, sem_send_z, sem_send_zi,
    sem_send_y, sem_recv_y, sem_relay, sem_send_relay, sem_vx, sem_send_vx, sem_vy, sem_send_vy,
):
    expert = lax.axis_index("expert")
    dp = lax.axis_index("dp")
    z, core = expert // 2, expert % 2
    y, x = dp // NX, dp % NX
    top, tokens = routes.shape[1], routes.shape[2]
    width = grads.shape[2] // NX
    slots, hidden_units = hidden.shape[2], hidden.shape[3]
    owned = hidden_units // (NX * NY)
    block = owned * NX
    half = width // 2
    cap = slots // (2 * NZ)

    def at_x(k):
        return {"dp": y * NX + k}

    def at_y(k):
        return {"dp": k * NX + x}

    def at_z(k):
        return {"expert": k * 2 + core}

    sibling = {"expert": z * 2 + 1 - core}

    def remote(src, dst, send, recv, where):
        return pltpu.make_async_remote_copy(
            src_ref=src, dst_ref=dst, send_sem=send, recv_sem=recv, device_id=where, device_id_type=MESH
        )

    def columns(k):
        return pl.ds(pl.multiple_of(k * width, width), width)

    local_tok = pltpu.make_async_copy(
        grads.at[0, :, columns(x)],
        tok.at[core * NZ + z, pl.ds(pl.multiple_of(x * tokens, tokens), tokens)],
        sem_local.at[0],
    )
    local_tok.start()
    local_hid = pltpu.make_async_copy(
        hidden.at[0, 0], hid.at[pl.ds(pl.multiple_of(x * slots, slots), slots)], sem_local.at[1]
    )
    local_hid.start()
    local_m1 = pltpu.make_async_copy(first_prev.at[0], mom1, sem_local.at[2])
    local_m1.start()
    local_m2 = pltpu.make_async_copy(second_prev.at[0], mom2, sem_local.at[3])
    local_m2.start()

    barrier = pltpu.get_barrier_semaphore()
    for k in range(1, NX):
        pl.semaphore_signal(barrier, inc=1, device_id=at_x((x + k) % NX), device_id_type=MESH)
    for k in range(1, NY):
        pl.semaphore_signal(barrier, inc=1, device_id=at_y((y + k) % NY), device_id_type=MESH)
    for k in (1, NZ - 1):
        pl.semaphore_signal(barrier, inc=1, device_id=at_z((z + k) % NZ), device_id_type=MESH)
    pl.semaphore_signal(barrier, inc=1, device_id=sibling, device_id_type=MESH)

    lane = iota((tokens, 128), 1)
    token = iota((tokens, 128), 0)
    place_routes = (lane == x * tokens + token).astype(F32)
    place_gates = (lane == NX * tokens + x * tokens + token).astype(F32)
    info_x[x] = jnp.dot(routes[0].astype(F32), place_routes, preferred_element_type=F32) + jnp.dot(
        gates[0], place_gates, preferred_element_type=F32, precision=HIGHEST
    )
    pl.semaphore_wait(barrier, NX - 1 + NY - 1 + 3)

    here = core * NZ + z
    my_rows = pl.ds(pl.multiple_of(x * tokens, tokens), tokens)
    my_slots = pl.ds(pl.multiple_of(x * slots, slots), slots)
    x_copies = []
    for k in (1, 3, 2):
        peer = (x + k) % NX
        x_copies.append(remote(info_x.at[x], info_x.at[x], sem_send_x.at[0, k], sem_info_x.at[x], at_x(peer)))
        x_copies.append(
            remote(
                grads.at[0, :, columns(peer)], tok.at[here, my_rows], sem_send_x.at[1, k], sem_tok_x.at[x], at_x(peer)
            )
        )
    for copy in x_copies:
        copy.start()
    for k in (1, 3, 2):
        peer = (x + k) % NX
        copy = remote(hidden.at[0, 0], hid.at[my_slots], sem_send_x.at[2, k], sem_hid.at[x], at_x(peer))
        copy.start()
        x_copies.append(copy)

    def rows_of(i):
        return pl.ds(pl.multiple_of(((x + i) % NX) * tokens, tokens), tokens)

    def tok_copy(zz, i, where, recv):
        ref = tok.at[core * NZ + zz, rows_of(i)]
        return remote(ref, ref, sem_send_z, recv, where)

    def info_copy(zz, where, recv):
        ref = info.at[core * NZ + zz]
        return remote(ref, ref, sem_send_zi, recv, where)

    right, left = at_z((z + 1) % NZ), at_z((z + NZ - 1) % NZ)

    def send_tok(zz, i, to_right, to_left):
        if to_right:
            tok_copy(zz, i, right, sem_z.at[zz, i]).start()
        if to_left:
            tok_copy(zz, i, left, sem_z.at[zz, i]).start()
        tok_copy(zz, i, sibling, sem_sib).start()

    def send_info(zz, to_right, to_left):
        if to_right:
            info_copy(zz, right, sem_z_info.at[zz]).start()
        if to_left:
            info_copy(zz, left, sem_z_info.at[zz]).start()
        info_copy(zz, sibling, sem_sib_info).start()

    local_tok.wait()
    send_tok(z, 0, True, True)
    for k in (1, 3, 2):
        peer = (x + k) % NX
        remote(info_x.at[peer], info_x.at[peer], sem_send_x.at[0, k], sem_info_x.at[peer], at_x(peer)).wait_recv()
    info[here] = info_x[0] + info_x[1] + info_x[2] + info_x[3]
    send_info(z, True, True)
    for i in (1, 3, 2):
        peer = (x + i) % NX
        arrived = tok.at[here, rows_of(i)]
        remote(arrived, arrived, sem_send_x.at[1, i], sem_tok_x.at[peer], at_x(peer)).wait_recv()
        send_tok(z, i, True, True)

    order = (0, 1, 3, 2)

    def z_step(d, right_subs, left_subs, right_info, left_info, right_on, left_on, right_info_on, left_info_on):
        from_left = (z + NZ - d) % NZ
        from_right = (z + d) % NZ
        if right_info:
            info_copy(from_left, right, sem_z_info.at[from_left]).wait_recv()
            send_info(from_left, right_info_on, False)
        if left_info:
            info_copy(from_right, left, sem_z_info.at[from_right]).wait_recv()
            send_info(from_right, False, left_info_on)
        for i in order:
            if i in right_subs:
                tok_copy(from_left, i, right, sem_z.at[from_left, i]).wait_recv()
                send_tok(from_left, i, i in right_on, False)
            if i in left_subs:
                tok_copy(from_right, i, left, sem_z.at[from_right, i]).wait_recv()
                send_tok(from_right, i, False, i in left_on)

    def z_loop(d, carry):
        z_step(d, order, order, True, True, order, order, True, True)
        return carry

    lax.fori_loop(1, NZ // 2 - 1, z_loop, 0)
    z_step(NZ // 2 - 1, order, order, True, True, (0, 1), (3, 2), True, False)
    z_step(NZ // 2, (0, 1), (3, 2), True, False, (), (), False, False)

    local_hid.wait()
    for k in (1, 3, 2):
        peer = (x + k) % NX
        arrived = hid.at[pl.ds(pl.multiple_of(peer * slots, slots), slots)]
        remote(arrived, arrived, sem_send_x.at[2, k], sem_hid.at[peer], at_x(peer)).wait_recv()
    for k in range(NX * slots // 128):
        hid_t[:, 128 * k : 128 * (k + 1)] = hid[128 * k : 128 * (k + 1), :].T

    theirs = pl.ds(pl.multiple_of((1 - core) * NZ, NZ), NZ)
    remote(info.at[theirs], info.at[theirs], sem_send_zi, sem_sib_info, sibling).wait_recv()
    sources = 2 * NZ
    both = info[...]
    lanes3 = iota(both.shape, 2)
    hit = jnp.logical_and(both == expert.astype(F32), lanes3 < NX * tokens)
    weights = pltpu.roll(both.reshape(sources * top, 128), 128 - NX * tokens, 1).reshape(both.shape)
    named = jnp.sum(jnp.where(hit, 1.0, 0.0), axis=1)
    gate = jnp.sum(jnp.where(hit, weights, 0.0), axis=1)
    before_row, before_col = iota((128, 128), 0), iota((128, 128), 1)
    before = jnp.where(
        jnp.logical_and(before_row < before_col, before_row // tokens == before_col // tokens), 1.0, 0.0
    )
    place = jnp.dot(named.astype(BF16), before.astype(BF16), preferred_element_type=F32)
    row_of = iota(named.shape, 0)
    source = 2 * (row_of % NZ) + row_of // NZ
    target = jnp.where(named > 0.5, place + (cap * source).astype(F32), -1.0)
    count = jnp.sum(named, axis=0, keepdims=True)
    lane1 = iota(count.shape, 1)

    all_tokens = sources * tokens
    spread_row, spread_lane = iota((128, all_tokens), 0), iota((128, all_tokens), 1)
    own_row = iota((sources, all_tokens), 0) == iota((sources, all_tokens), 1) // tokens
    slot_id = iota((slots, all_tokens), 0).astype(F32)
    remote(tok.at[theirs], tok.at[theirs], sem_send_z, sem_sib, sibling).wait_recv()
    total = jnp.zeros((1, 1), F32)
    for r in range(NX):
        routed = jnp.sum(jnp.where(lane1 // tokens == r, count, 0.0), axis=1, keepdims=True)
        total = total + jnp.floor((routed + (PAD - 1.0)) * (1.0 / PAD)) * PAD
        repeat = jnp.where(spread_row == r * tokens + spread_lane % tokens, 1.0, 0.0)
        target_r = jnp.dot(target.astype(BF16), repeat.astype(BF16), preferred_element_type=F32)
        gate_r = jnp.dot(gate, repeat, preferred_element_type=F32, precision=HIGHEST)
        target_r = jnp.sum(jnp.where(own_row, target_r, 0.0), axis=0, keepdims=True)
        gate_r = jnp.sum(jnp.where(own_row, gate_r, 0.0), axis=0, keepdims=True)
        chosen = slot_id == target_r
        gate_col = jnp.sum(jnp.where(chosen, gate_r, 0.0), axis=1, keepdims=True)
        rows = tok[:, tokens * r : tokens * (r + 1), :].reshape(all_tokens, width)
        picked = jnp.dot(jnp.where(chosen, 1.0, 0.0).astype(BF16), rows, preferred_element_type=F32)
        sent[slots * r : slots * (r + 1), :] = (picked * gate_col).astype(BF16)

    up, down = at_y((y + 1) % NY), at_y((y + NY - 1) % NY)
    chains = ((0, 4), (0, 3), (1, 3), (1, 4))

    def block_of(k, h):
        return part[k, :, half * h : half * (h + 1)]

    def y_copy(c, k):
        return remote(
            send_y.at[c, k], recv_y.at[c, k], sem_send_y.at[c, k], sem_recv_y.at[c, k], down if c % 2 else up
        )

    def y_send(c, k):
        h, length = chains[c]
        far = length - k
        dest = (y + NY - far) % NY if c % 2 else (y + far) % NY
        value = block_of(dest, h)
        if k:
            y_copy(c, k - 1).wait_recv()
            value = value + recv_y[c, k - 1].astype(F32)
        send_y[c, k] = value.astype(BF16)
        y_copy(c, k).start()

    for h in range(2):
        part[:, :, half * h : half * (h + 1)] = jnp.dot(
            hid_t[...], sent[:, half * h : half * (h + 1)], preferred_element_type=F32
        ).reshape(NY, block, half)
        for c in (2 * h, 2 * h + 1):
            y_send(c, 0)
    spread = jnp.zeros((1, 1), F32)
    for r in range(NX):
        rows = pl.ds(slots * r, slots)
        over = (((1,), (1,)), ((), ()))
        gram_h = lax.dot_general(hid[rows, :], hid[rows, :], over, preferred_element_type=F32)
        gram_s = lax.dot_general(sent[rows, :], sent[rows, :], over, preferred_element_type=F32)
        both_grams = jnp.sum(gram_h * gram_s, axis=1, keepdims=True)
        spread = spread + jnp.sum(both_grams, axis=0, keepdims=True)
    for k in range(1, 4):
        for c in (0, 3, 1, 2):
            if k < chains[c][1]:
                y_send(c, k)
    for h in range(2):
        value = block_of(y, h)
        for c in (2 * h, 2 * h + 1):
            last = chains[c][1] - 1
            y_copy(c, last).wait_recv()
            value = value + recv_y[c, last].astype(F32)
        own[:, half * h : half * (h + 1)] = value

    relay_copies = []
    for k in (2, 1, 3):
        peer = (x + k) % NX
        rows = pl.ds(pl.multiple_of(peer * owned, 8), owned)
        copy = remote(own.at[rows], relay.at[x], sem_send_relay.at[k], sem_relay.at[x], at_x(peer))
        copy.start()
        relay_copies.append(copy)
    relay[x] = own[pl.ds(pl.multiple_of(x * owned, 8), owned), :]
    summed = own[...]
    power = jnp.sum(jnp.sum(summed * summed, axis=0, keepdims=True), axis=1, keepdims=True)
    sub = iota((8, 128), 0)
    vec_x[x] = jnp.where(
        sub == 0, power, jnp.where(sub == 1, spread, jnp.where(sub == 2, total * (1.0 / NX), 0.0))
    )
    for k in (2, 1, 3):
        copy = remote(vec_x.at[x], vec_x.at[x], sem_send_vx.at[k], sem_vx.at[x], at_x((x + k) % NX))
        copy.start()
        relay_copies.append(copy)
    for k in (1, 3, 2):
        peer = (x + k) % NX
        remote(vec_x.at[peer], vec_x.at[peer], sem_send_vx.at[k], sem_vx.at[peer], at_x(peer)).wait_recv()
    vec_y[y] = vec_x[0] + vec_x[1] + vec_x[2] + vec_x[3]
    for k in (4, 3, 5, 2, 6, 1, 7):
        copy = remote(vec_y.at[y], vec_y.at[y], sem_send_vy.at[k], sem_vy.at[y], at_y((y + k) % NY))
        copy.start()
        relay_copies.append(copy)
    local_m1.wait()
    local_m2.wait()
    for k in (1, 3, 2):
        peer = (x + k) % NX
        remote(relay.at[peer], relay.at[peer], sem_send_relay.at[k], sem_relay.at[peer], at_x(peer)).wait_recv()
    for k in range(1, NY):
        peer = (y + k) % NY
        remote(vec_y.at[peer], vec_y.at[peer], sem_send_vy.at[k], sem_vy.at[peer], at_y(peer)).wait_recv()
    scalars = vec_y[0]
    for k in range(1, NY):
        scalars = scalars + vec_y[k]
    power, spread, total = scalars[0:1, 0:1], scalars[1:2, 0:1], scalars[2:3, 0:1]
    replicas = float(NX * NY)
    noise = total * spread / (replicas * power + 1e-06)
    lr_scale = noise / (noise + total / replicas)
    lr_out[0] = lr_scale[0, 0]
    for k in range(NX):
        cols = pl.ds(width * k, width)
        mean = relay[k] / total
        first = 0.9 * mom1[:, cols] + 0.1 * mean
        second = 0.95 * mom2[:, cols] + 0.05 * mean * mean
        out[0, :, cols] = (
            -lr_scale
            * (first / (1.0 - 0.9**ADAM_STEP))
            / (jnp.sqrt(second / (1.0 - 0.95**ADAM_STEP)) + 1e-08)
        )

    for copy in x_copies + relay_copies:
        copy.wait_send()
    sent_blocks = tok.at[pl.ds(0, 31)]
    remote(sent_blocks, sent_blocks, sem_send_z, sem_sib, sibling).wait_send()
    sent_infos = info.at[pl.ds(0, 31)]
    remote(sent_infos, sent_infos, sem_send_zi, sem_sib_info, sibling).wait_send()
    for c in range(4):
        for k in range(chains[c][1]):
            y_copy(c, k).wait_send()


def on_device(out_grad, routes, gate_probs, hidden, first_prev, second_prev):
    routes = jnp.swapaxes(routes, 1, 2)
    gate_probs = jnp.swapaxes(gate_probs, 1, 2)
    tokens, width = out_grad.shape[1], out_grad.shape[2] // NX
    slots, units = hidden.shape[2:]
    owned = units // (NX * NY)
    block, half = owned * NX, width // 2
    dma = pltpu.SemaphoreType.DMA
    any_space = pl.BlockSpec(memory_space=pl.ANY)
    vmem = pl.BlockSpec(memory_space=pltpu.VMEM)
    return pl.pallas_call(
        kernel,
        out_shape=(
            jax.ShapeDtypeStruct(first_prev.shape, F32),
            jax.ShapeDtypeStruct((1,), F32),
        ),
        in_specs=[any_space, vmem, vmem, any_space, any_space, any_space],
        out_specs=(vmem, pl.BlockSpec(memory_space=pltpu.SMEM)),
        scratch_shapes=[
            pltpu.VMEM((2 * NZ, NX * tokens, width), BF16),
            pltpu.VMEM((2 * NZ, 8, 128), F32),
            pltpu.VMEM((NX, 8, 128), F32),
            pltpu.VMEM((NX * slots, units), BF16),
            pltpu.VMEM((units, NX * slots), BF16),
            pltpu.VMEM((NX * slots, width), BF16),
            pltpu.VMEM((NY, block, width), F32),
            pltpu.VMEM((4, 4, block, half), BF16),
            pltpu.VMEM((4, 4, block, half), BF16),
            pltpu.VMEM((block, width), F32),
            pltpu.VMEM((NX, owned, width), F32),
            pltpu.VMEM((NX, 8, 128), F32),
            pltpu.VMEM((NY, 8, 128), F32),
            pltpu.VMEM(first_prev.shape[1:], F32),
            pltpu.VMEM(first_prev.shape[1:], F32),
            dma((4,)),
            dma((NX,)),
            dma((NX,)),
            dma((NX,)),
            dma((3, NX)),
            dma((NZ, NX)),
            dma((NZ,)),
            dma,
            dma,
            dma,
            dma,
            dma((4, 4)),
            dma((4, 4)),
            dma((NX,)),
            dma((NX,)),
            dma((NX,)),
            dma((NX,)),
            dma((NY,)),
            dma((NY,)),
        ],
        compiler_params=pltpu.CompilerParams(
            collective_id=0, has_side_effects=True, vmem_limit_bytes=40 * 1024 * 1024
        ),
    )(out_grad, routes, gate_probs, hidden, first_prev, second_prev)


def solution(mesh):
    return jax.shard_map(
        on_device,
        mesh=mesh,
        in_specs=(
            P("dp", "expert", None),
            P("dp", "expert", None),
            P("dp", "expert", None),
            P("dp", "expert", None, None),
            P("expert", "dp", None),
            P("expert", "dp", None),
        ),
        out_specs=(P("expert", "dp", None), P("expert")),
        check_vma=False,
    )
```

```python
import jax
import jax.numpy as jnp
from jax import lax
from jax.experimental import pallas as pl
from jax.experimental.pallas import tpu as pltpu
from jax.sharding import PartitionSpec as P

PAD = 16
ADAM_STEP = 3
MESH = pl.DeviceIdType.MESH
NX, NY, NZ = 4, 8, 16
HIGHEST = lax.Precision.HIGHEST
F32 = jnp.float32
BF16 = jnp.bfloat16


def iota(shape, dim):
    return lax.broadcasted_iota(jnp.int32, shape, dim)


def kernel(
    grads, routes_in, gates_in, hidden, first_prev, second_prev,
    out, lr_out,
    tok, info, info_y, info_own, hid, hid_pass, hid_t, sent, part, send_x, recv_x, own, relay, vec, mom1, mom2,
    routes, gates,
    sem_local, sem_tok, sem_send_tok, sem_info, sem_send_info,
    sem_z, sem_z_info, sem_send_z, sem_send_zi, sem_sib, sem_sib_info, sem_send_sib, sem_send_sibi,
    sem_hand, sem_send_hand, sem_h, sem_send_h, sem_sib_h, sem_send_sib_h,
    sem_x, sem_send_x, sem_relay, sem_send_relay, sem_vec, sem_send_vec,
):
    expert = lax.axis_index("expert")
    dp = lax.axis_index("dp")
    z, core = expert // 2, expert % 2
    y, x = dp // NX, dp % NX
    tokens = routes_in.shape[2]
    width = grads.shape[2] // NY
    slots, units = hidden.shape[2], hidden.shape[3]
    owned = units // (NX * NY)
    cap = slots // (2 * NZ)
    sources = 2 * NZ
    all_tokens = sources * tokens
    quarter = NY * tokens // 2
    half = slots // 2

    def at_x(k):
        return {"dp": y * NX + k}

    def at_y(k):
        return {"dp": k * NX + x}

    def at_z(k):
        return {"expert": k * 2 + core}

    def core1_at_y(k):
        return {"expert": z * 2 + 1, "dp": k * NX + x}

    sibling = {"expert": z * 2 + 1 - core}

    def remote(src, dst, send, recv, where):
        return pltpu.make_async_remote_copy(
            src_ref=src, dst_ref=dst, send_sem=send, recv_sem=recv, device_id=where, device_id_type=MESH
        )

    def arrived(ref, sem):
        remote(ref, ref, sem_send_hand, sem, sibling).wait_recv()

    def left(ref, sem):
        remote(ref, ref, sem, sem_hand, sibling).wait_send()

    def columns(k):
        return pl.ds(pl.multiple_of(k * width, width), width)

    def rows(k, count):
        return pl.ds(pl.multiple_of(k * count, count), count)

    local = [
        pltpu.make_async_copy(routes_in, routes, sem_local.at[0]),
        pltpu.make_async_copy(gates_in, gates, sem_local.at[1]),
        pltpu.make_async_copy(hidden.at[0, 0], hid.at[y], sem_local.at[2]),
        pltpu.make_async_copy(first_prev.at[0], mom1, sem_local.at[3]),
        pltpu.make_async_copy(second_prev.at[0], mom2, sem_local.at[4]),
    ]
    for copy in local:
        copy.start()

    barrier = pltpu.get_barrier_semaphore()

    def greet(where):
        pl.semaphore_signal(barrier, inc=1, device_id=where, device_id_type=MESH)

    greet(sibling)
    for k in range(1, NY):
        greet({"expert": z * 2 + 1 - core, "dp": ((y + k) % NY) * NX + x})
    for k in range(1, NX * NY):
        greet({"dp": (dp + k) % (NX * NY)})

    @pl.when(core == 1)
    def _():
        greet(at_z((z + 1) % NZ))
        greet(at_z((z + NZ - 1) % NZ))
        pl.semaphore_wait(barrier, NX * NY - 1 + NY + 2)

    @pl.when(core == 0)
    def _():
        pl.semaphore_wait(barrier, NX * NY - 1 + NY)

    my_rows = rows(y, tokens)
    for k in range(1, NY):
        peer = (y + k) % NY
        remote(
            grads.at[0, :, columns(peer)], tok.at[expert, my_rows], sem_send_tok, sem_tok.at[core, y // 4],
            core1_at_y(peer),
        ).start()

    @pl.when(core == 0)
    def _():
        remote(
            grads.at[0, :, columns(y)], tok.at[expert, my_rows], sem_send_tok, sem_tok.at[core, y // 4], sibling
        ).start()

    @pl.when(core == 1)
    def _():
        pltpu.make_async_copy(grads.at[0, :, columns(y)], tok.at[expert, my_rows], sem_tok.at[core, y // 4]).start()
        remote(hidden.at[0, 0], hid_pass.at[y], sem_send_hand, sem_hand, sibling).start()

    up, down = at_y((y + 1) % NY), at_y((y + NY - 1) % NY)

    def hid_copy(e, r, h, where, first=False):
        held = hid_pass if e else hid
        ref = held.at[r, pl.ds(half * h, half)]
        src = hidden.at[0, 0, pl.ds(half * h, half)] if first and not e else ref
        return remote(src, ref, sem_send_h.at[e], sem_h.at[r, e, h], where)

    @pl.when(core == 0)
    def _():
        for h in range(2):
            hid_copy(0, y, h, up, True).start()
            hid_copy(0, y, h, down, True).start()

    place_lanes = (iota((tokens, 128), 1) == y * tokens + iota((tokens, 128), 0)).astype(F32)
    local[0].wait()
    local[1].wait()
    info_own[0:8] = jnp.dot(routes[0].astype(F32), place_lanes, preferred_element_type=F32)
    info_own[8:16] = jnp.dot(gates[0], place_lanes, preferred_element_type=F32, precision=HIGHEST)
    mine = core * NY + y
    for k in range(1, NY):
        remote(info_own, info_y.at[mine], sem_send_info, sem_info, core1_at_y((y + k) % NY)).start()

    @pl.when(core == 0)
    def _():
        remote(info_own, info_y.at[mine], sem_send_info, sem_info, sibling).start()

        def hand_over(r, h):
            ref = hid_pass.at[r, pl.ds(half * h, half)]
            remote(ref, hid.at[r, pl.ds(half * h, half)], sem_send_sib_h, sem_sib_h, sibling).start()

        arrived(hid_pass.at[y], sem_hand)
        for h in range(2):
            hid_copy(1, y, h, up).start()
            hid_copy(1, y, h, down).start()
        for d in range(1, 5):
            below, above = (y + NY - d) % NY, (y + d) % NY
            for e in range(2):
                for h in range(2):
                    if d < 4 or e == 0:
                        hid_copy(e, below, h, up).wait_recv()
                        if d < 3 or (d == 3 and e == 0):
                            hid_copy(e, below, h, up).start()
                        if e == 1:
                            hand_over(below, h)
                    if d < 4 or e == 1:
                        hid_copy(e, above, h, down).wait_recv()
                        if d < 3 or (d == 3 and e == 1):
                            hid_copy(e, above, h, down).start()
                        if e == 1:
                            hand_over(above, h)
        local[2].wait()

    subs = ((1, 0), (1, 1), (0, 0), (0, 1))

    @pl.when(core == 1)
    def _():
        right, left_ = at_z((z + 1) % NZ), at_z((z + NZ - 1) % NZ)

        def tok_ref(zz, c, h):
            return tok.at[2 * zz + c, pl.ds(quarter * h, quarter)]

        def tok_copy(zz, c, h, where):
            ref = tok_ref(zz, c, h)
            return remote(ref, ref, sem_send_z, sem_z.at[zz, 2 * c + h], where)

        def tok_share(zz, c, h):
            ref = tok_ref(zz, c, h)
            remote(ref, ref, sem_send_sib, sem_sib, sibling).start()

        def info_ref(zz):
            return info.at[pl.ds(pl.multiple_of(2 * zz, 2), 2)]

        def info_copy(zz, where):
            return remote(info_ref(zz), info_ref(zz), sem_send_zi, sem_z_info.at[zz], where)

        def info_share(zz):
            remote(info_ref(zz), info_ref(zz), sem_send_sibi, sem_sib_info, sibling).start()

        for c, h in subs:
            arrived(tok_ref(z, c, h), sem_tok.at[c, h])
            tok_copy(z, c, h, right).start()
            tok_copy(z, c, h, left_).start()
            tok_share(z, c, h)
        arrived(info_y.at[pl.ds(0, 2 * NY - 1)], sem_info)
        info_y[mine] = info_own[...]
        for c in range(2):
            total_info = info_y[c * NY]
            for k in range(1, NY):
                total_info = total_info + info_y[c * NY + k]
            info[2 * z + c] = total_info
        info_copy(z, right).start()
        info_copy(z, left_).start()
        info_share(z)

        def z_step(d, last):
            from_left, from_right = (z + NZ - d) % NZ, (z + d) % NZ
            for c, h in subs:
                if last < 2 or c == 1:
                    tok_copy(from_left, c, h, right).wait_recv()
                    if last == 0 or (last == 1 and c == 1):
                        tok_copy(from_left, c, h, right).start()
                    tok_share(from_left, c, h)
                if last < 2 or c == 0:
                    tok_copy(from_right, c, h, left_).wait_recv()
                    if last == 0 or (last == 1 and c == 0):
                        tok_copy(from_right, c, h, left_).start()
                    tok_share(from_right, c, h)
            info_copy(from_left, right).wait_recv()
            if last < 2:
                info_copy(from_left, right).start()
            info_share(from_left)
            if last < 2:
                info_copy(from_right, left_).wait_recv()
                if last == 0:
                    info_copy(from_right, left_).start()
                info_share(from_right)

        def z_loop(d, carry):
            z_step(d, 0)
            return carry

        lax.fori_loop(1, NZ // 2 - 1, z_loop, 0)
        z_step(NZ // 2 - 1, 1)
        z_step(NZ // 2, 2)
        local[2].wait()
        arrived(hid.at[pl.ds(0, NY - 1)], sem_sib_h)

    for k in range(NY * slots // 128):
        first, last = 128 * k // slots, (128 * k + 127) // slots
        begin = 128 * k - first * slots
        if first == last:
            piece = hid[first, begin : begin + 128, :]
        else:
            cut = slots - begin
            piece = jnp.concatenate([hid[first, begin:slots, :], hid[last, 0 : 128 - cut, :]], axis=0)
        hid_t[:, 128 * k : 128 * (k + 1)] = piece.T

    @pl.when(core == 0)
    def _():
        arrived(info, sem_sib_info)

    both = info[...]
    hit = both[:, 0:8, :] == expert.astype(F32)
    named = jnp.sum(jnp.where(hit, 1.0, 0.0), axis=1)
    gate = jnp.sum(jnp.where(hit, both[:, 8:16, :], 0.0), axis=1)
    from_row, to_col = iota((128, 128), 0), iota((128, 128), 1)
    same = from_row // tokens == to_col // tokens
    before = jnp.where(jnp.logical_and(same, from_row < to_col), 1.0, 0.0).astype(BF16)
    place = jnp.dot(named.astype(BF16), before, preferred_element_type=F32)
    target = jnp.where(named > 0.5, place + (cap * iota(named.shape, 0)).astype(F32), -1.0).astype(BF16)
    count = jnp.sum(named, axis=0, keepdims=True)
    routed = jnp.dot(
        jnp.broadcast_to(count, (8, 128)).astype(BF16), jnp.where(same, 1.0, 0.0).astype(BF16),
        preferred_element_type=F32,
    )[0:1]
    padded = jnp.floor((routed + (PAD - 1.0)) * (1.0 / PAD)) * PAD
    total = jnp.sum(padded, axis=1, keepdims=True) * (1.0 / tokens)

    lane_row, lane_col = iota((128, all_tokens), 0), iota((128, all_tokens), 1)
    own_row = iota((sources, all_tokens), 0) == iota((sources, all_tokens), 1) // tokens
    slot_id = iota((slots, all_tokens), 0).astype(F32)

    @pl.when(core == 0)
    def _():
        arrived(tok, sem_sib)

    for r in range(NY):
        repeat = jnp.where(lane_row == r * tokens + lane_col % tokens, 1.0, 0.0)
        target_r = jnp.dot(target, repeat.astype(BF16), preferred_element_type=F32)
        gate_r = jnp.dot(gate, repeat, preferred_element_type=F32, precision=HIGHEST)
        target_r = jnp.sum(jnp.where(own_row, target_r, 0.0), axis=0, keepdims=True)
        gate_r = jnp.sum(jnp.where(own_row, gate_r, 0.0), axis=0, keepdims=True)
        chosen = slot_id == target_r
        gate_col = jnp.sum(jnp.where(chosen, gate_r, 0.0), axis=1, keepdims=True)
        block = tok[:, tokens * r : tokens * (r + 1), :].reshape(all_tokens, width)
        picked = jnp.dot(jnp.where(chosen, 1.0, 0.0).astype(BF16), block, preferred_element_type=F32)
        sent[slots * r : slots * (r + 1), :] = (picked * gate_col).astype(BF16)

    part[...] = jnp.dot(hid_t[...], sent[...], preferred_element_type=F32).reshape(NY, NX, owned, width)
    for k in (2, 1, 3):
        peer = (x + k) % NX
        send_x[peer] = part[:, peer].reshape(NY * owned, width).astype(BF16)
        remote(send_x.at[peer], recv_x.at[x], sem_send_x.at[k], sem_x.at[x], at_x(peer)).start()

    over = (((1,), (1,)), ((), ()))
    spread = jnp.zeros((1, 1), F32)
    for r in range(NY):
        sent_r = sent[slots * r : slots * (r + 1), :]
        gram_h = lax.dot_general(hid[r], hid[r], over, preferred_element_type=F32)
        gram_s = lax.dot_general(sent_r, sent_r, over, preferred_element_type=F32)
        both_grams = jnp.sum(gram_h * gram_s, axis=0, keepdims=True)
        spread = spread + jnp.sum(both_grams, axis=1, keepdims=True)

    summed = part[:, x].reshape(NY * owned, width)
    for k in (1, 3, 2):
        peer = (x + k) % NX
        arrived(recv_x.at[peer], sem_x.at[peer])
        summed = summed + recv_x[peer].astype(F32)
    own[...] = summed

    power = jnp.sum(jnp.sum(summed * summed, axis=0, keepdims=True), axis=1, keepdims=True)
    sub = iota((8, 128), 0)
    vec[dp] = jnp.where(
        sub == 0, power, jnp.where(sub == 1, spread, jnp.where(sub == 2, total * (1.0 / NY), 0.0))
    )
    for k in (4, 3, 5, 2, 6, 1, 7):
        for i in range(NX):
            peer = ((y + k) % NY) * NX + (x + i) % NX
            remote(vec.at[dp], vec.at[dp], sem_send_vec, sem_vec, {"dp": peer}).start()
    for i in range(1, NX):
        remote(vec.at[dp], vec.at[dp], sem_send_vec, sem_vec, at_x((x + i) % NX)).start()
    for k in (4, 3, 5, 2, 6, 1, 7):
        peer = (y + k) % NY
        remote(own.at[rows(peer, owned)], relay.at[y], sem_send_relay, sem_relay, at_y(peer)).start()
    relay[y] = own[rows(y, owned), :]
    local[3].wait()
    local[4].wait()
    arrived(relay.at[pl.ds(0, NY - 1)], sem_relay)
    arrived(vec.at[pl.ds(0, NX * NY - 1)], sem_vec)
    scalars = vec[0]
    for k in range(1, NX * NY):
        scalars = scalars + vec[k]
    power, spread, total = scalars[0:1, 0:1], scalars[1:2, 0:1], scalars[2:3, 0:1]
    replicas = float(NX * NY)
    noise = total * spread / (replicas * power + 1e-06)
    lr_scale = noise / (noise + total / replicas)
    lr_out[0] = lr_scale[0, 0]
    for k in range(NY):
        cols = pl.ds(width * k, width)
        mean = relay[k] / total
        first = 0.9 * mom1[:, cols] + 0.1 * mean
        second = 0.95 * mom2[:, cols] + 0.05 * mean * mean
        out[0, :, cols] = (
            -lr_scale
            * (first / (1.0 - 0.9**ADAM_STEP))
            / (jnp.sqrt(second / (1.0 - 0.95**ADAM_STEP)) + 1e-08)
        )

    tok_flat = tok.at[0, pl.ds(0, tokens * (NY - 1))]
    left(tok_flat, sem_send_tok)
    left(info_y.at[pl.ds(0, NY - 1)], sem_send_info)
    for k in (2, 1, 3):
        left(send_x.at[(x + k) % NX], sem_send_x.at[k])
    left(relay.at[pl.ds(0, NY - 1)], sem_send_relay)
    left(vec.at[pl.ds(0, NX * NY - 1)], sem_send_vec)

    @pl.when(core == 0)
    def _():
        left(tok.at[0, pl.ds(0, tokens)], sem_send_tok)
        left(info_y.at[0], sem_send_info)
        for e in range(2):
            left(hid.at[pl.ds(0, NY - 1)], sem_send_h.at[e])
        left(hid.at[pl.ds(0, NY - 1)], sem_send_sib_h)

    @pl.when(core == 1)
    def _():
        left(hid.at[0], sem_send_hand)
        left(tok.at[pl.ds(0, 30)], sem_send_z)
        left(tok, sem_send_sib)
        left(info.at[pl.ds(0, 30)], sem_send_zi)
        left(info, sem_send_sibi)


def on_device(out_grad, routes, gate_probs, hidden, first_prev, second_prev):
    routes = jnp.swapaxes(routes, 1, 2)
    gate_probs = jnp.swapaxes(gate_probs, 1, 2)
    tokens, width = out_grad.shape[1], out_grad.shape[2] // NY
    slots, units = hidden.shape[2:]
    owned = units // (NX * NY)
    dma = pltpu.SemaphoreType.DMA
    hbm = pl.BlockSpec(memory_space=pltpu.HBM)
    vmem = pl.BlockSpec(memory_space=pltpu.VMEM)
    return pl.pallas_call(
        kernel,
        out_shape=(
            jax.ShapeDtypeStruct(first_prev.shape, F32),
            jax.ShapeDtypeStruct((1,), F32),
        ),
        in_specs=[hbm] * 6,
        out_specs=(vmem, pl.BlockSpec(memory_space=pltpu.SMEM)),
        scratch_shapes=[
            pltpu.VMEM((2 * NZ, NY * tokens, width), BF16),
            pltpu.VMEM((2 * NZ, 16, 128), F32),
            pltpu.VMEM((2 * NY, 16, 128), F32),
            pltpu.VMEM((16, 128), F32),
            pltpu.VMEM((NY, slots, units), BF16),
            pltpu.VMEM((NY, slots, units), BF16),
            pltpu.VMEM((units, NY * slots), BF16),
            pltpu.VMEM((NY * slots, width), BF16),
            pltpu.VMEM((NY, NX, owned, width), F32),
            pltpu.VMEM((NX, NY * owned, width), BF16),
            pltpu.VMEM((NX, NY * owned, width), BF16),
            pltpu.VMEM((NY * owned, width), F32),
            pltpu.VMEM((NY, owned, width), F32),
            pltpu.VMEM((NX * NY, 8, 128), F32),
            pltpu.VMEM(first_prev.shape[1:], F32),
            pltpu.VMEM(first_prev.shape[1:], F32),
            pltpu.VMEM(routes.shape, jnp.int32),
            pltpu.VMEM(routes.shape, F32),
            dma((5,)),
            dma((2, 2)),
            dma,
            dma,
            dma,
            dma((NZ, 4)),
            dma((NZ,)),
            dma,
            dma,
            dma,
            dma,
            dma,
            dma,
            dma,
            dma,
            dma((NY, 2, 2)),
            dma((2,)),
            dma,
            dma,
            dma((NX,)),
            dma((NX,)),
            dma,
            dma,
            dma,
            dma,
        ],
        compiler_params=pltpu.CompilerParams(
            collective_id=0, has_side_effects=True, vmem_limit_bytes=60 * 1024 * 1024
        ),
    )(out_grad, routes, gate_probs, hidden, first_prev, second_prev)


def solution(mesh):
    return jax.shard_map(
        on_device,
        mesh=mesh,
        in_specs=(
            P("dp", "expert", None),
            P("dp", "expert", None),
            P("dp", "expert", None),
            P("dp", "expert", None, None),
            P("expert", "dp", None),
            P("expert", "dp", None),
        ),
        out_specs=(P("expert", "dp", None), P("expert")),
        check_vma=False,
    )
```

```python
import jax
import jax.numpy as jnp
from jax import lax
from jax.experimental import pallas as pl
from jax.experimental.pallas import tpu as pltpu
from jax.sharding import PartitionSpec as P

PAD = 16
ADAM_STEP = 3
MESH = pl.DeviceIdType.MESH
NX, NY, NZ = 4, 8, 16
REACH = NZ // 2
HOPS = {0: (2, 1), 2: (2, 1), 4: (2, 1), 6: (2, 1)}
ORDER = (2, 1, 4, 3, 6, 5, 8, 7)
HIGHEST = lax.Precision.HIGHEST
F32 = jnp.float32
BF16 = jnp.bfloat16


def iota(shape, dim):
    return lax.broadcasted_iota(jnp.int32, shape, dim)


def kernel(
    grads, routes_in, gates_in, hidden, first_prev, second_prev,
    out, lr_out,
    tok, info, info_y, info_own, grads_here, hid, hid_pass, hid_t, sent, part, send_x, recv_x, own, relay, vec, norms, mom1, mom2,
    routes, gates,
    sem_local, sem_tok, sem_send_tok, sem_info, sem_send_info,
    sem_z, sem_z_info, sem_send_z, sem_send_zi, sem_sib, sem_sib_info, sem_send_sib, sem_send_sibi,
    sem_hand, sem_send_hand, sem_h, sem_send_h, sem_sib_h, sem_send_sib_h,
    sem_x, sem_send_x, sem_relay, sem_send_relay, sem_vec, sem_send_vec, sem_norms, sem_send_norms,
):
    expert = lax.axis_index("expert")
    dp = lax.axis_index("dp")
    z, core = expert // 2, expert % 2
    y, x = dp // NX, dp % NX
    tokens = routes_in.shape[2]
    width = grads.shape[2] // NY
    slots, units = hidden.shape[2], hidden.shape[3]
    owned = units // (NX * NY)
    cap = slots // (2 * NZ)
    sources = 2 * NZ
    all_tokens = sources * tokens
    quarter = NY * tokens // 2
    half = slots // 2

    def at_x(k):
        return {"dp": y * NX + k}

    def at_y(k):
        return {"dp": k * NX + x}

    def at_z(k):
        return {"expert": k * 2 + core}

    def core1_at_y(k):
        return {"expert": z * 2 + 1, "dp": k * NX + x}

    sibling = {"expert": z * 2 + 1 - core}

    def remote(src, dst, send, recv, where):
        return pltpu.make_async_remote_copy(
            src_ref=src, dst_ref=dst, send_sem=send, recv_sem=recv, device_id=where, device_id_type=MESH
        )

    def arrived(ref, sem):
        remote(ref, ref, sem_send_hand, sem, sibling).wait_recv()

    def left(ref, sem):
        remote(ref, ref, sem, sem_hand, sibling).wait_send()

    def columns(k):
        return pl.ds(pl.multiple_of(k * width, width), width)

    def rows(k, count):
        return pl.ds(pl.multiple_of(k * count, count), count)

    local = [
        pltpu.make_async_copy(routes_in, routes, sem_local.at[0]),
        pltpu.make_async_copy(gates_in, gates, sem_local.at[1]),
        pltpu.make_async_copy(hidden.at[0, 0], hid.at[y], sem_local.at[2]),
        pltpu.make_async_copy(first_prev.at[0], mom1, sem_local.at[3]),
        pltpu.make_async_copy(second_prev.at[0], mom2, sem_local.at[4]),
        pltpu.make_async_copy(grads.at[0], grads_here, sem_local.at[5]),
    ]
    for copy in local:
        copy.start()

    barrier = pltpu.get_barrier_semaphore()

    def greet(where):
        pl.semaphore_signal(barrier, inc=1, device_id=where, device_id_type=MESH)

    greet(sibling)
    for k in range(1, NY):
        greet({"expert": z * 2 + 1 - core, "dp": ((y + k) % NY) * NX + x})
    for k in range(1, NX * NY):
        greet({"dp": (dp + k) % (NX * NY)})

    @pl.when(core == 1)
    def _():
        for k in (1, 2, NZ - 2, NZ - 1):
            greet(at_z((z + k) % NZ))

    lane_of = iota((tokens, 128), 1) % tokens == iota((tokens, 128), 0)
    spread_out = jnp.where(lane_of, 1.0, 0.0)
    choice = iota((8, 128), 0) == iota((8, 128), 1) // tokens
    local[0].wait()
    local[1].wait()
    wide = jnp.dot(routes[0].astype(F32), spread_out, preferred_element_type=F32)
    info_own[0:1] = jnp.sum(jnp.where(choice, wide, 0.0), axis=0, keepdims=True)
    wide = jnp.dot(gates[0], spread_out, preferred_element_type=F32, precision=HIGHEST)
    info_own[1:2] = jnp.sum(jnp.where(choice, wide, 0.0), axis=0, keepdims=True)

    @pl.when(core == 1)
    def _():
        pl.semaphore_wait(barrier, NX * NY - 1 + NY + 4)

    @pl.when(core == 0)
    def _():
        pl.semaphore_wait(barrier, NX * NY - 1 + NY)

    my_rows = rows(y, tokens)
    local[5].wait()
    for k in range(1, NY):
        peer = (y + k) % NY
        remote(
            grads_here.at[:, columns(peer)], tok.at[expert, my_rows], sem_send_tok, sem_tok.at[core, y // 4],
            core1_at_y(peer),
        ).start()

    @pl.when(core == 0)
    def _():
        remote(
            grads_here.at[:, columns(y)], tok.at[expert, my_rows], sem_send_tok, sem_tok.at[core, y // 4], sibling
        ).start()

    @pl.when(core == 1)
    def _():
        pltpu.make_async_copy(grads_here.at[:, columns(y)], tok.at[expert, my_rows], sem_tok.at[core, y // 4]).start()
        remote(hidden.at[0, 0], hid_pass.at[y], sem_send_hand, sem_hand, sibling).start()

    up, down = at_y((y + 1) % NY), at_y((y + NY - 1) % NY)

    def hid_copy(e, r, h, where, first=False):
        held = hid_pass if e else hid
        ref = held.at[r, pl.ds(half * h, half)]
        src = hidden.at[0, 0, pl.ds(half * h, half)] if first and not e else ref
        return remote(src, ref, sem_send_h.at[e], sem_h.at[r, e, h], where)

    @pl.when(core == 0)
    def _():
        for h in range(2):
            hid_copy(0, y, h, up, True).start()
            hid_copy(0, y, h, down, True).start()

    for k in range(1, NY):
        remote(info_own, info_y.at[core * NY + y], sem_send_info, sem_info, core1_at_y((y + k) % NY)).start()

    @pl.when(core == 0)
    def _():
        remote(info_own, info_y.at[core * NY + y], sem_send_info, sem_info, sibling).start()

        def hand_over(r, h):
            ref = hid_pass.at[r, pl.ds(half * h, half)]
            remote(ref, hid.at[r, pl.ds(half * h, half)], sem_send_sib_h, sem_sib_h, sibling).start()

        arrived(hid_pass.at[y], sem_hand)
        for h in range(2):
            hid_copy(1, y, h, up).start()
            hid_copy(1, y, h, down).start()
        for d in range(1, 5):
            below, above = (y + NY - d) % NY, (y + d) % NY
            for e in range(2):
                for h in range(2):
                    if d < 4 or e == 0:
                        hid_copy(e, below, h, up).wait_recv()
                        if d < 3 or (d == 3 and e == 0):
                            hid_copy(e, below, h, up).start()
                        if e == 1:
                            hand_over(below, h)
                    if d < 4 or e == 1:
                        hid_copy(e, above, h, down).wait_recv()
                        if d < 3 or (d == 3 and e == 1):
                            hid_copy(e, above, h, down).start()
                        if e == 1:
                            hand_over(above, h)
        local[2].wait()

    subs = ((1, 0), (1, 1), (0, 0), (0, 1))

    @pl.when(core == 1)
    def _():
        right = [at_z((z + k) % NZ) for k in (1, 2)]
        left_ = [at_z((z + NZ - k) % NZ) for k in (1, 2)]

        def tok_ref(zz, c, h):
            return tok.at[2 * zz + c, pl.ds(quarter * h, quarter)]

        def tok_copy(zz, c, h, where):
            ref = tok_ref(zz, c, h)
            return remote(ref, ref, sem_send_z, sem_z.at[zz, 2 * c + h], where)

        def tok_share(zz, c, h):
            ref = tok_ref(zz, c, h)
            remote(ref, ref, sem_send_sib, sem_sib, sibling).start()

        def info_ref(zz):
            return info.at[pl.ds(pl.multiple_of(2 * zz, 2), 2)]

        def info_copy(zz, where):
            return remote(info_ref(zz), info_ref(zz), sem_send_zi, sem_z_info.at[zz], where)

        def info_share(zz):
            remote(info_ref(zz), info_ref(zz), sem_send_sibi, sem_sib_info, sibling).start()

        def tok_send(zz, c, h, where):
            for there in where:
                tok_copy(zz, c, h, there).start()

        def info_send(zz, where):
            for there in where:
                info_copy(zz, there).start()

        for c, h in subs:
            arrived(tok_ref(z, c, h), sem_tok.at[c, h])
            tok_send(z, c, h, [way[k - 1] for k in HOPS[0] for way in (right, left_)])
            tok_share(z, c, h)
        info_y[core * NY + y] = info_own[...]
        arrived(info_y.at[pl.ds(0, 2 * NY - 1)], sem_info)
        for c in range(2):
            for i in range(2):
                info[2 * z + c, NY * i : NY * (i + 1)] = info_y[NY * c : NY * (c + 1), i, :]
        info_send(z, [way[k - 1] for k in HOPS[0] for way in (right, left_)])
        info_share(z)

        def receive(d):
            on = HOPS.get(d, ())
            from_left, from_right = (z + NZ - d) % NZ, (z + d) % NZ
            ways = ((from_left, right, 1), (from_right, left_, 0))
            for c, h in subs:
                for source, where, far_core in ways:
                    if d < REACH or c == far_core:
                        tok_copy(source, c, h, where[0]).wait_recv()
                        tok_send(source, c, h, [where[k - 1] for k in on if d + k < REACH or c == far_core])
                        tok_share(source, c, h)
            for source, where, far_core in ways:
                if d < REACH or far_core == 1:
                    info_copy(source, where[0]).wait_recv()
                    info_send(source, [where[k - 1] for k in on if d + k < REACH or far_core == 1])
                    info_share(source)

        for d in ORDER:
            receive(d)
        local[2].wait()
        arrived(hid.at[pl.ds(0, NY - 1)], sem_sib_h)

    for k in range(NY * slots // 128):
        first, last = 128 * k // slots, (128 * k + 127) // slots
        begin = 128 * k - first * slots
        if first == last:
            piece = hid[first, begin : begin + 128, :]
        else:
            cut = slots - begin
            piece = jnp.concatenate([hid[first, begin:slots, :], hid[last, 0 : 128 - cut, :]], axis=0)
        hid_t[:, 128 * k : 128 * (k + 1)] = piece.T

    @pl.when(core == 0)
    def _():
        arrived(info, sem_sib_info)

    pairs = sources * NY
    both = info[...]
    hit = both[:, 0:NY, :].reshape(pairs, 128) == expert.astype(F32)
    fold = jnp.where(iota((128, 128), 0) % tokens == iota((128, 128), 1), 1.0, 0.0)
    named = jnp.dot(jnp.where(hit, 1.0, 0.0).astype(BF16), fold.astype(BF16), preferred_element_type=F32)
    gate = jnp.dot(
        jnp.where(hit, both[:, NY : 2 * NY, :].reshape(pairs, 128), 0.0), fold, preferred_element_type=F32,
        precision=HIGHEST,
    )
    before = jnp.where(iota((128, 128), 0) < iota((128, 128), 1), 1.0, 0.0).astype(BF16)
    place = jnp.dot(named.astype(BF16), before, preferred_element_type=F32)
    target = jnp.where(named > 0.5, place + (cap * (iota(named.shape, 0) // NY)).astype(F32), -1.0)
    by_replica = jnp.sum(named.reshape(sources, NY, 128), axis=0)
    routed = jnp.sum(by_replica, axis=1, keepdims=True)
    padded = jnp.floor((routed + (PAD - 1.0)) * (1.0 / PAD)) * PAD
    total = jnp.sum(padded, axis=0, keepdims=True)
    repeat = jnp.where(iota((128, all_tokens), 0) == iota((128, all_tokens), 1) % tokens, 1.0, 0.0)
    target = jnp.dot(target.astype(BF16), repeat.astype(BF16), preferred_element_type=F32)
    gate = jnp.dot(gate, repeat, preferred_element_type=F32, precision=HIGHEST)
    own_row = iota((sources, NY, all_tokens), 0) == iota((sources, NY, all_tokens), 2) // tokens
    target = jnp.sum(jnp.where(own_row, target.reshape(own_row.shape), 0.0), axis=0)
    gate = jnp.sum(jnp.where(own_row, gate.reshape(own_row.shape), 0.0), axis=0)
    slot_id = iota((slots, all_tokens), 0).astype(F32)

    @pl.when(core == 0)
    def _():
        arrived(tok, sem_sib)

    for r in range(NY):
        target_r, gate_r = target[r : r + 1], gate[r : r + 1]
        chosen = slot_id == target_r
        gate_col = jnp.sum(jnp.where(chosen, gate_r, 0.0), axis=1, keepdims=True)
        block = tok[:, tokens * r : tokens * (r + 1), :].reshape(all_tokens, width)
        picked = jnp.dot(jnp.where(chosen, 1.0, 0.0).astype(BF16), block, preferred_element_type=F32)
        sent[slots * r : slots * (r + 1), :] = (picked * gate_col).astype(BF16)

    part[...] = jnp.dot(hid_t[...], sent[...], preferred_element_type=F32).reshape(NY, NX, owned, width)
    for k in (2, 1, 3):
        peer = (x + k) % NX
        send_x[peer] = part[:, peer].reshape(NY * owned, width).astype(BF16)
        remote(send_x.at[peer], recv_x.at[x], sem_send_x.at[k], sem_x.at[x], at_x(peer)).start()

    over = (((1,), (1,)), ((), ()))
    spread = jnp.zeros((1, 1), F32)
    for r in range(NY):
        sent_r = sent[slots * r : slots * (r + 1), :]
        gram_h = lax.dot_general(hid[r], hid[r], over, preferred_element_type=F32)
        gram_s = lax.dot_general(sent_r, sent_r, over, preferred_element_type=F32)
        both_grams = jnp.sum(gram_h * gram_s, axis=0, keepdims=True)
        spread = spread + jnp.sum(both_grams, axis=1, keepdims=True)

    sub = iota((2, 128), 0)
    vec[dp] = jnp.where(sub == 0, spread, total * (1.0 / NY))

    def to_all(ref, send, recv):
        for k in (4, 3, 5, 2, 6, 1, 7):
            for i in range(NX):
                peer = ((y + k) % NY) * NX + (x + i) % NX
                remote(ref, ref, send, recv, {"dp": peer}).start()
        for i in range(1, NX):
            remote(ref, ref, send, recv, at_x((x + i) % NX)).start()

    to_all(vec.at[dp], sem_send_vec, sem_vec)

    summed = part[:, x].reshape(NY * owned, width)
    for k in (1, 3, 2):
        peer = (x + k) % NX
        arrived(recv_x.at[peer], sem_x.at[peer])
        summed = summed + recv_x[peer].astype(F32)

    power = jnp.sum(jnp.sum(summed * summed, axis=0, keepdims=True), axis=1, keepdims=True)
    norms[dp] = jnp.broadcast_to(power, (1, 128))
    to_all(norms.at[dp], sem_send_norms, sem_norms)
    for k in range(NY):
        piece = summed[owned * k : owned * (k + 1), :]
        own[k] = jnp.concatenate([piece[:, : width // 2], piece[:, width // 2 :]], axis=0).astype(BF16)
    for k in (4, 3, 5, 2, 6, 1, 7):
        peer = (y + k) % NY
        remote(own.at[peer], relay.at[y], sem_send_relay, sem_relay, at_y(peer)).start()
    relay[y] = own[y]
    local[3].wait()
    local[4].wait()
    arrived(vec.at[pl.ds(0, NX * NY - 1)], sem_vec)
    scalars = vec[0]
    for k in range(1, NX * NY):
        scalars = scalars + vec[k]
    spread, total = scalars[0:1, 0:1], scalars[1:2, 0:1]
    arrived(relay.at[pl.ds(0, NY - 1)], sem_relay)
    for k in range(NY):
        rows_k = relay[k].astype(F32)
        for h in range(2):
            cols = pl.ds(width * k + width // 2 * h, width // 2)
            mean = rows_k[owned * h : owned * (h + 1)] / total
            first = 0.9 * mom1[:, cols] + 0.1 * mean
            second = 0.95 * mom2[:, cols] + 0.05 * mean * mean
            mom1[:, cols] = (first / (1.0 - 0.9**ADAM_STEP)) / (
                jnp.sqrt(second / (1.0 - 0.95**ADAM_STEP)) + 1e-08
            )
    arrived(norms.at[pl.ds(0, NX * NY - 1)], sem_norms)
    power = norms[0]
    for k in range(1, NX * NY):
        power = power + norms[k]
    power = power[:, 0:1]
    replicas = float(NX * NY)
    noise = total * spread / (replicas * power + 1e-06)
    lr_scale = noise / (noise + total / replicas)
    lr_out[0] = lr_scale[0, 0]
    out[0] = -lr_scale * mom1[...]

    tok_flat = tok.at[0, pl.ds(0, tokens * (NY - 1))]
    left(tok_flat, sem_send_tok)
    left(info_y.at[pl.ds(0, NY - 1)], sem_send_info)
    for k in (2, 1, 3):
        left(send_x.at[(x + k) % NX], sem_send_x.at[k])
    left(relay.at[pl.ds(0, NY - 1)], sem_send_relay)
    left(vec.at[pl.ds(0, NX * NY - 1)], sem_send_vec)
    left(norms.at[pl.ds(0, NX * NY - 1)], sem_send_norms)

    @pl.when(core == 0)
    def _():
        left(tok.at[0, pl.ds(0, tokens)], sem_send_tok)
        left(info_y.at[0], sem_send_info)
        for e in range(2):
            left(hid.at[pl.ds(0, NY - 1)], sem_send_h.at[e])
        left(hid.at[pl.ds(0, NY - 1)], sem_send_sib_h)

    @pl.when(core == 1)
    def _():
        left(hid.at[0], sem_send_hand)
        left(tok.at[pl.ds(0, 30)], sem_send_z)
        left(tok, sem_send_sib)
        left(info.at[pl.ds(0, 30)], sem_send_zi)
        left(info, sem_send_sibi)


def on_device(out_grad, routes, gate_probs, hidden, first_prev, second_prev):
    routes = jnp.swapaxes(routes, 1, 2)
    gate_probs = jnp.swapaxes(gate_probs, 1, 2)
    tokens, width = out_grad.shape[1], out_grad.shape[2] // NY
    slots, units = hidden.shape[2:]
    owned = units // (NX * NY)
    dma = pltpu.SemaphoreType.DMA
    hbm = pl.BlockSpec(memory_space=pltpu.HBM)
    vmem = pl.BlockSpec(memory_space=pltpu.VMEM)
    return pl.pallas_call(
        kernel,
        out_shape=(
            jax.ShapeDtypeStruct(first_prev.shape, F32),
            jax.ShapeDtypeStruct((1,), F32),
        ),
        in_specs=[hbm] * 6,
        out_specs=(vmem, pl.BlockSpec(memory_space=pltpu.SMEM)),
        scratch_shapes=[
            pltpu.VMEM((2 * NZ, NY * tokens, width), BF16),
            pltpu.VMEM((2 * NZ, 2 * NY, 128), F32),
            pltpu.VMEM((2 * NY, 2, 128), F32),
            pltpu.VMEM((2, 128), F32),
            pltpu.VMEM(out_grad.shape[1:], BF16),
            pltpu.VMEM((NY, slots, units), BF16),
            pltpu.VMEM((NY, slots, units), BF16),
            pltpu.VMEM((units, NY * slots), BF16),
            pltpu.VMEM((NY * slots, width), BF16),
            pltpu.VMEM((NY, NX, owned, width), F32),
            pltpu.VMEM((NX, NY * owned, width), BF16),
            pltpu.VMEM((NX, NY * owned, width), BF16),
            pltpu.VMEM((NY, 2 * owned, width // 2), BF16),
            pltpu.VMEM((NY, 2 * owned, width // 2), BF16),
            pltpu.VMEM((NX * NY, 2, 128), F32),
            pltpu.VMEM((NX * NY, 1, 128), F32),
            pltpu.VMEM(first_prev.shape[1:], F32),
            pltpu.VMEM(first_prev.shape[1:], F32),
            pltpu.VMEM(routes.shape, jnp.int32),
            pltpu.VMEM(routes.shape, F32),
            dma((6,)),
            dma((2, 2)),
            dma,
            dma,
            dma,
            dma((NZ, 4)),
            dma((NZ,)),
            dma,
            dma,
            dma,
            dma,
            dma,
            dma,
            dma,
            dma,
            dma((NY, 2, 2)),
            dma((2,)),
            dma,
            dma,
            dma((NX,)),
            dma((NX,)),
            dma,
            dma,
            dma,
            dma,
            dma,
            dma,
        ],
        compiler_params=pltpu.CompilerParams(
            collective_id=0, has_side_effects=True, vmem_limit_bytes=60 * 1024 * 1024
        ),
    )(out_grad, routes, gate_probs, hidden, first_prev, second_prev)


def solution(mesh):
    return jax.shard_map(
        on_device,
        mesh=mesh,
        in_specs=(
            P("dp", "expert", None),
            P("dp", "expert", None),
            P("dp", "expert", None),
            P("dp", "expert", None, None),
            P("expert", "dp", None),
            P("expert", "dp", None),
        ),
        out_specs=(P("expert", "dp", None), P("expert")),
        check_vma=False,
    )
```

```python
import jax
import jax.numpy as jnp
from jax import lax
from jax.experimental import pallas as pl
from jax.experimental.pallas import tpu as pltpu
from jax.sharding import PartitionSpec as P

PAD = 16
ADAM_STEP = 3
MESH = pl.DeviceIdType.MESH
NX, NY, NZ = 4, 8, 16
REACH = NZ // 2
NEAR_FIRST = (1, 7, 6, 4, 5, 3, 2)
HOPS = {0: (2, 1), 2: (2, 1), 4: (2, 1), 6: (2, 1)}
ORDER = (2, 1, 4, 3, 6, 5, 8, 7)
HIGHEST = lax.Precision.HIGHEST
F32 = jnp.float32
BF16 = jnp.bfloat16


def iota(shape, dim):
    return lax.broadcasted_iota(jnp.int32, shape, dim)


def kernel(
    grads, routes_in, gates_in, hidden, first_prev, second_prev,
    ratio, lr_out,
    tok, info, info_y, info_own, grads_here, hid, hid_pass, hid_t, sent, part, send_x, recv_x, own, relay, vec, norms, mom1, mom2,
    routes, gates,
    sem_local, sem_tok, sem_send_tok, sem_info, sem_send_info,
    sem_z, sem_z_info, sem_send_z, sem_send_zi, sem_sib, sem_sib_info, sem_send_sib, sem_send_sibi,
    sem_hand, sem_send_hand, sem_h, sem_send_h, sem_sib_h, sem_send_sib_h,
    sem_x, sem_send_x, sem_relay, sem_send_relay, sem_vec, sem_send_vec, sem_norms, sem_send_norms,
):
    expert = lax.axis_index("expert")
    dp = lax.axis_index("dp")
    z, core = expert // 2, expert % 2
    y, x = dp // NX, dp % NX
    tokens = routes_in.shape[2]
    width = grads.shape[2] // NY
    slots, units = hidden.shape[2], hidden.shape[3]
    owned = units // (NX * NY)
    cap = slots // (2 * NZ)
    sources = 2 * NZ
    all_tokens = sources * tokens
    quarter = NY * tokens // 2
    half = slots // 2

    def at_x(k):
        return {"dp": y * NX + k}

    def at_y(k):
        return {"dp": k * NX + x}

    def at_z(k):
        return {"expert": k * 2 + core}

    def core1_at_y(k):
        return {"expert": z * 2 + 1, "dp": k * NX + x}

    sibling = {"expert": z * 2 + 1 - core}

    def remote(src, dst, send, recv, where):
        return pltpu.make_async_remote_copy(
            src_ref=src, dst_ref=dst, send_sem=send, recv_sem=recv, device_id=where, device_id_type=MESH
        )

    def arrived(ref, sem):
        remote(ref, ref, sem_send_hand, sem, sibling).wait_recv()

    def left(ref, sem):
        remote(ref, ref, sem, sem_hand, sibling).wait_send()

    def columns(k):
        return pl.ds(pl.multiple_of(k * width, width), width)

    def rows(k, count):
        return pl.ds(pl.multiple_of(k * count, count), count)

    local = [
        pltpu.make_async_copy(routes_in, routes, sem_local.at[0]),
        pltpu.make_async_copy(gates_in, gates, sem_local.at[1]),
        pltpu.make_async_copy(hidden.at[0, 0], hid.at[y], sem_local.at[2]),
        pltpu.make_async_copy(first_prev.at[0], mom1, sem_local.at[3]),
        pltpu.make_async_copy(second_prev.at[0], mom2, sem_local.at[4]),
        pltpu.make_async_copy(grads.at[0], grads_here, sem_local.at[5]),
    ]
    for copy in local:
        copy.start()

    barrier = pltpu.get_barrier_semaphore()

    def greet(where):
        pl.semaphore_signal(barrier, inc=1, device_id=where, device_id_type=MESH)

    greet(sibling)
    for k in range(1, NY):
        greet({"expert": z * 2 + 1 - core, "dp": ((y + k) % NY) * NX + x})
    for k in range(1, NX * NY):
        greet({"dp": (dp + k) % (NX * NY)})

    @pl.when(core == 1)
    def _():
        for k in (1, 2, NZ - 2, NZ - 1):
            greet(at_z((z + k) % NZ))

    lane_of = iota((tokens, 128), 1) % tokens == iota((tokens, 128), 0)
    spread_out = jnp.where(lane_of, 1.0, 0.0)
    choice = iota((8, 128), 0) == iota((8, 128), 1) // tokens
    local[0].wait()
    local[1].wait()
    wide = jnp.dot(routes[0].astype(F32), spread_out, preferred_element_type=F32)
    info_own[0:1] = jnp.sum(jnp.where(choice, wide, 0.0), axis=0, keepdims=True)
    wide = jnp.dot(gates[0], spread_out, preferred_element_type=F32, precision=HIGHEST)
    info_own[1:2] = jnp.sum(jnp.where(choice, wide, 0.0), axis=0, keepdims=True)

    @pl.when(core == 1)
    def _():
        pl.semaphore_wait(barrier, NX * NY - 1 + NY + 4)

    @pl.when(core == 0)
    def _():
        pl.semaphore_wait(barrier, NX * NY - 1 + NY)

    local[5].wait()

    def token_send(k, where):
        place = (1 - k) % NY
        remote(
            grads_here.at[:, columns((y + k) % NY)], tok.at[expert, pl.ds(place * tokens, tokens)], sem_send_tok,
            sem_tok.at[core, 2 * place // NY], where,
        ).start()

    @pl.when(core == 0)
    def _():
        token_send(0, sibling)

    for k in NEAR_FIRST:
        token_send(k, core1_at_y((y + k) % NY))

    @pl.when(core == 1)
    def _():
        pltpu.make_async_copy(grads_here.at[:, columns(y)], tok.at[expert, pl.ds(tokens, tokens)], sem_tok.at[core, 0]).start()
        remote(hidden.at[0, 0], hid_pass.at[y], sem_send_hand, sem_hand, sibling).start()

    up, down = at_y((y + 1) % NY), at_y((y + NY - 1) % NY)

    def hid_copy(e, r, h, where, first=False):
        held = hid_pass if e else hid
        ref = held.at[r, pl.ds(half * h, half)]
        src = hidden.at[0, 0, pl.ds(half * h, half)] if first and not e else ref
        return remote(src, ref, sem_send_h.at[e], sem_h.at[r, e, h], where)

    @pl.when(core == 0)
    def _():
        for h in range(2):
            hid_copy(0, y, h, up, True).start()
            hid_copy(0, y, h, down, True).start()

    for k in NEAR_FIRST:
        remote(
            info_own, info_y.at[core * NY + (1 - k) % NY], sem_send_info, sem_info, core1_at_y((y + k) % NY)
        ).start()

    @pl.when(core == 0)
    def _():
        remote(info_own, info_y.at[core * NY + 1], sem_send_info, sem_info, sibling).start()

        def hand_over(r, h):
            ref = hid_pass.at[r, pl.ds(half * h, half)]
            remote(ref, hid.at[r, pl.ds(half * h, half)], sem_send_sib_h, sem_sib_h, sibling).start()

        arrived(hid_pass.at[y], sem_hand)
        for h in range(2):
            hid_copy(1, y, h, up).start()
            hid_copy(1, y, h, down).start()
        for d in range(1, 5):
            below, above = (y + NY - d) % NY, (y + d) % NY
            for e in range(2):
                for h in range(2):
                    if d < 4 or e == 0:
                        hid_copy(e, below, h, up).wait_recv()
                        if d < 3 or (d == 3 and e == 0):
                            hid_copy(e, below, h, up).start()
                        if e == 1:
                            hand_over(below, h)
                    if d < 4 or e == 1:
                        hid_copy(e, above, h, down).wait_recv()
                        if d < 3 or (d == 3 and e == 1):
                            hid_copy(e, above, h, down).start()
                        if e == 1:
                            hand_over(above, h)
        local[2].wait()

    subs = ((1, 0), (0, 0), (1, 1), (0, 1))

    @pl.when(core == 1)
    def _():
        right = [at_z((z + k) % NZ) for k in (1, 2)]
        left_ = [at_z((z + NZ - k) % NZ) for k in (1, 2)]

        def tok_ref(zz, c, h):
            return tok.at[2 * zz + c, pl.ds(quarter * h, quarter)]

        def tok_copy(zz, c, h, where):
            ref = tok_ref(zz, c, h)
            return remote(ref, ref, sem_send_z, sem_z.at[zz, 2 * c + h], where)

        def tok_share(zz, c, h):
            ref = tok_ref(zz, c, h)
            remote(ref, ref, sem_send_sib, sem_sib, sibling).start()

        def info_ref(zz):
            return info.at[pl.ds(pl.multiple_of(2 * zz, 2), 2)]

        def info_copy(zz, where):
            return remote(info_ref(zz), info_ref(zz), sem_send_zi, sem_z_info.at[zz], where)

        def info_share(zz):
            remote(info_ref(zz), info_ref(zz), sem_send_sibi, sem_sib_info, sibling).start()

        def tok_send(zz, c, h, where):
            for there in where:
                tok_copy(zz, c, h, there).start()

        def info_send(zz, where):
            for there in where:
                info_copy(zz, there).start()

        for c, h in subs:
            arrived(tok_ref(z, c, h), sem_tok.at[c, h])
            tok_send(z, c, h, [way[k - 1] for k in HOPS[0] for way in (right, left_)])
            tok_share(z, c, h)
        info_y[core * NY + 1] = info_own[...]
        arrived(info_y.at[pl.ds(0, 2 * NY - 1)], sem_info)
        for c in range(2):
            for i in range(2):
                info[2 * z + c, NY * i : NY * (i + 1)] = info_y[NY * c : NY * (c + 1), i, :]
        info_send(z, [way[k - 1] for k in HOPS[0] for way in (right, left_)])
        info_share(z)

        def receive(d):
            on = HOPS.get(d, ())
            from_left, from_right = (z + NZ - d) % NZ, (z + d) % NZ
            ways = ((from_left, right, 1), (from_right, left_, 0))
            for c, h in subs:
                for source, where, far_core in ways:
                    if d < REACH or c == far_core:
                        tok_copy(source, c, h, where[0]).wait_recv()
                        tok_send(source, c, h, [where[k - 1] for k in on if d + k < REACH or c == far_core])
                        tok_share(source, c, h)
            for source, where, far_core in ways:
                if d < REACH or far_core == 1:
                    info_copy(source, where[0]).wait_recv()
                    info_send(source, [where[k - 1] for k in on if d + k < REACH or far_core == 1])
                    info_share(source)

        for d in ORDER:
            receive(d)
        local[2].wait()
        arrived(hid.at[pl.ds(0, NY - 1)], sem_sib_h)

    def hid_at(place):
        return (y + NY - 1 + place) % NY

    for k in range(NY * slots // 128):
        first, last = 128 * k // slots, (128 * k + 127) // slots
        begin = 128 * k - first * slots
        if first == last:
            piece = hid[hid_at(first), begin : begin + 128, :]
        else:
            cut = slots - begin
            piece = jnp.concatenate([hid[hid_at(first), begin:slots, :], hid[hid_at(last), 0 : 128 - cut, :]], axis=0)
        piece = piece.astype(F32).T.reshape(NY, NX, owned, 128)
        for i in range(NX):
            hid_t[i, :, 128 * k : 128 * (k + 1)] = piece[:, i].reshape(NY * owned, 128).astype(BF16)

    @pl.when(core == 0)
    def _():
        arrived(info, sem_sib_info)

    pairs = sources * NY
    both = info[...]
    hit = both[:, 0:NY, :].reshape(pairs, 128) == expert.astype(F32)
    fold = jnp.where(iota((128, 128), 0) % tokens == iota((128, 128), 1), 1.0, 0.0)
    named = jnp.dot(jnp.where(hit, 1.0, 0.0).astype(BF16), fold.astype(BF16), preferred_element_type=F32)
    gate = jnp.dot(
        jnp.where(hit, both[:, NY : 2 * NY, :].reshape(pairs, 128), 0.0), fold, preferred_element_type=F32,
        precision=HIGHEST,
    )
    before = jnp.where(iota((128, 128), 0) < iota((128, 128), 1), 1.0, 0.0).astype(BF16)
    place = jnp.dot(named.astype(BF16), before, preferred_element_type=F32)
    target = jnp.where(named > 0.5, place + (cap * (iota(named.shape, 0) // NY)).astype(F32), -1.0)
    by_replica = jnp.sum(named.reshape(sources, NY, 128), axis=0)
    routed = jnp.sum(by_replica, axis=1, keepdims=True)
    padded = jnp.floor((routed + (PAD - 1.0)) * (1.0 / PAD)) * PAD
    total = jnp.sum(padded, axis=0, keepdims=True)
    repeat = jnp.where(iota((128, all_tokens), 0) == iota((128, all_tokens), 1) % tokens, 1.0, 0.0)
    target = jnp.dot(target.astype(BF16), repeat.astype(BF16), preferred_element_type=F32)
    gate = jnp.dot(gate, repeat, preferred_element_type=F32, precision=HIGHEST)
    own_row = iota((sources, NY, all_tokens), 0) == iota((sources, NY, all_tokens), 2) // tokens
    target = jnp.sum(jnp.where(own_row, target.reshape(own_row.shape), 0.0), axis=0)
    gate = jnp.sum(jnp.where(own_row, gate.reshape(own_row.shape), 0.0), axis=0)
    slot_id = iota((slots, all_tokens), 0).astype(F32)

    @pl.when(core == 0)
    def _():
        arrived(tok, sem_sib)

    for r in range(NY):
        target_r, gate_r = target[r : r + 1], gate[r : r + 1]
        chosen = slot_id == target_r
        gate_col = jnp.sum(jnp.where(chosen, gate_r, 0.0), axis=1, keepdims=True)
        block = tok[:, tokens * r : tokens * (r + 1), :].reshape(all_tokens, width)
        picked = jnp.dot(jnp.where(chosen, 1.0, 0.0).astype(BF16), block, preferred_element_type=F32)
        sent[slots * r : slots * (r + 1), :] = (picked * gate_col).astype(BF16)

    def x_send(k, rows_of):
        peer = (x + k) % NX
        send_x[peer] = rows_of.astype(BF16)
        remote(send_x.at[peer], recv_x.at[x], sem_send_x.at[k], sem_x.at[x], at_x(peer)).start()

    for pair in ((2, 1), (3, 0)):
        hid_rows = jnp.concatenate([hid_t[(x + k) % NX] for k in pair], axis=0)
        product = jnp.dot(hid_rows, sent[...], preferred_element_type=F32)
        for i, k in enumerate(pair):
            rows_of = product[NY * owned * i : NY * owned * (i + 1)]
            if k:
                x_send(k, rows_of)
            else:
                part[...] = rows_of

    over = (((1,), (1,)), ((), ()))
    spread = jnp.zeros((1, 1), F32)
    for r in range(NY):
        sent_r = sent[slots * r : slots * (r + 1), :]
        hid_r = hid[hid_at(r)]
        gram_h = lax.dot_general(hid_r, hid_r, over, preferred_element_type=F32)
        gram_s = lax.dot_general(sent_r, sent_r, over, preferred_element_type=F32)
        both_grams = jnp.sum(gram_h * gram_s, axis=0, keepdims=True)
        spread = spread + jnp.sum(both_grams, axis=1, keepdims=True)

    sub = iota((2, 128), 0)
    vec[dp] = jnp.where(sub == 0, spread, total * (1.0 / NY))

    def to_all(ref, send, recv):
        for k in (4, 3, 5, 2, 6, 1, 7):
            for i in range(NX):
                peer = ((y + k) % NY) * NX + (x + i) % NX
                remote(ref, ref, send, recv, {"dp": peer}).start()
        for i in range(1, NX):
            remote(ref, ref, send, recv, at_x((x + i) % NX)).start()

    to_all(vec.at[dp], sem_send_vec, sem_vec)

    summed = part[...]
    for k in (1, 3, 2):
        peer = (x + k) % NX
        arrived(recv_x.at[peer], sem_x.at[peer])
        summed = summed + recv_x[peer].astype(F32)

    power = jnp.sum(jnp.sum(summed * summed, axis=0, keepdims=True), axis=1, keepdims=True)
    norms[dp] = jnp.broadcast_to(power, (1, 128))
    to_all(norms.at[dp], sem_send_norms, sem_norms)
    for k in range(NY):
        piece = summed[owned * k : owned * (k + 1), :]
        own[k] = jnp.concatenate([piece[:, : width // 2], piece[:, width // 2 :]], axis=0).astype(BF16)
    for k in (4, 3, 5, 2, 6, 1, 7):
        peer = (y + k) % NY
        remote(own.at[peer], relay.at[y], sem_send_relay, sem_relay, at_y(peer)).start()
    relay[y] = own[y]
    local[3].wait()
    local[4].wait()
    arrived(vec.at[pl.ds(0, NX * NY - 1)], sem_vec)
    scalars = vec[0]
    for k in range(1, NX * NY):
        scalars = scalars + vec[k]
    spread, total = scalars[0:1, 0:1], scalars[1:2, 0:1]
    arrived(relay.at[pl.ds(0, NY - 1)], sem_relay)
    for k in range(NY):
        rows_k = relay[k].astype(F32)
        for h in range(2):
            cols = pl.ds(width * k + width // 2 * h, width // 2)
            mean = rows_k[owned * h : owned * (h + 1)] / total
            first = 0.9 * mom1[:, cols] + 0.1 * mean
            second = 0.95 * mom2[:, cols] + 0.05 * mean * mean
            mom1[:, cols] = (first / (1.0 - 0.9**ADAM_STEP)) / (
                jnp.sqrt(second / (1.0 - 0.95**ADAM_STEP)) + 1e-08
            )
    write = pltpu.make_async_copy(mom1, ratio.at[0], sem_local.at[0])
    write.start()
    arrived(norms.at[pl.ds(0, NX * NY - 1)], sem_norms)
    power = norms[0]
    for k in range(1, NX * NY):
        power = power + norms[k]
    power = power[:, 0:1]
    replicas = float(NX * NY)
    noise = total * spread / (replicas * power + 1e-06)
    lr_scale = noise / (noise + total / replicas)
    lr_out[0] = lr_scale[0, 0]

    write.wait()
    tok_flat = tok.at[0, pl.ds(0, tokens * (NY - 1))]
    left(tok_flat, sem_send_tok)
    left(info_y.at[pl.ds(0, NY - 1)], sem_send_info)
    for k in (2, 1, 3):
        left(send_x.at[(x + k) % NX], sem_send_x.at[k])
    left(relay.at[pl.ds(0, NY - 1)], sem_send_relay)
    left(vec.at[pl.ds(0, NX * NY - 1)], sem_send_vec)
    left(norms.at[pl.ds(0, NX * NY - 1)], sem_send_norms)

    @pl.when(core == 0)
    def _():
        left(tok.at[0, pl.ds(0, tokens)], sem_send_tok)
        left(info_y.at[0], sem_send_info)
        for e in range(2):
            left(hid.at[pl.ds(0, NY - 1)], sem_send_h.at[e])
        left(hid.at[pl.ds(0, NY - 1)], sem_send_sib_h)

    @pl.when(core == 1)
    def _():
        left(hid.at[0], sem_send_hand)
        left(tok.at[pl.ds(0, 30)], sem_send_z)
        left(tok, sem_send_sib)
        left(info.at[pl.ds(0, 30)], sem_send_zi)
        left(info, sem_send_sibi)


def on_device(out_grad, routes, gate_probs, hidden, first_prev, second_prev):
    routes = jnp.swapaxes(routes, 1, 2)
    gate_probs = jnp.swapaxes(gate_probs, 1, 2)
    tokens, width = out_grad.shape[1], out_grad.shape[2] // NY
    slots, units = hidden.shape[2:]
    owned = units // (NX * NY)
    dma = pltpu.SemaphoreType.DMA
    hbm = pl.BlockSpec(memory_space=pltpu.HBM)
    ratio, lr_scale = pl.pallas_call(
        kernel,
        out_shape=(
            jax.ShapeDtypeStruct(first_prev.shape, F32),
            jax.ShapeDtypeStruct((1,), F32),
        ),
        in_specs=[hbm] * 6,
        out_specs=(hbm, pl.BlockSpec(memory_space=pltpu.SMEM)),
        scratch_shapes=[
            pltpu.VMEM((2 * NZ, NY * tokens, width), BF16),
            pltpu.VMEM((2 * NZ, 2 * NY, 128), F32),
            pltpu.VMEM((2 * NY, 2, 128), F32),
            pltpu.VMEM((2, 128), F32),
            pltpu.VMEM(out_grad.shape[1:], BF16),
            pltpu.VMEM((NY, slots, units), BF16),
            pltpu.VMEM((NY, slots, units), BF16),
            pltpu.VMEM((NX, NY * owned, NY * slots), BF16),
            pltpu.VMEM((NY * slots, width), BF16),
            pltpu.VMEM((NY * owned, width), F32),
            pltpu.VMEM((NX, NY * owned, width), BF16),
            pltpu.VMEM((NX, NY * owned, width), BF16),
            pltpu.VMEM((NY, 2 * owned, width // 2), BF16),
            pltpu.VMEM((NY, 2 * owned, width // 2), BF16),
            pltpu.VMEM((NX * NY, 2, 128), F32),
            pltpu.VMEM((NX * NY, 1, 128), F32),
            pltpu.VMEM(first_prev.shape[1:], F32),
            pltpu.VMEM(first_prev.shape[1:], F32),
            pltpu.VMEM(routes.shape, jnp.int32),
            pltpu.VMEM(routes.shape, F32),
            dma((6,)),
            dma((2, 2)),
            dma,
            dma,
            dma,
            dma((NZ, 4)),
            dma((NZ,)),
            dma,
            dma,
            dma,
            dma,
            dma,
            dma,
            dma,
            dma,
            dma((NY, 2, 2)),
            dma((2,)),
            dma,
            dma,
            dma((NX,)),
            dma((NX,)),
            dma,
            dma,
            dma,
            dma,
            dma,
            dma,
        ],
        compiler_params=pltpu.CompilerParams(
            collective_id=0, has_side_effects=True, vmem_limit_bytes=60 * 1024 * 1024
        ),
    )(out_grad, routes, gate_probs, hidden, first_prev, second_prev)
    return -lr_scale[0] * ratio, lr_scale


def solution(mesh):
    return jax.shard_map(
        on_device,
        mesh=mesh,
        in_specs=(
            P("dp", "expert", None),
            P("dp", "expert", None),
            P("dp", "expert", None),
            P("dp", "expert", None, None),
            P("expert", "dp", None),
            P("expert", "dp", None),
        ),
        out_specs=(P("expert", "dp", None), P("expert")),
        check_vma=False,
    )
```

```python
import jax
import jax.numpy as jnp
from jax import lax
from jax.experimental import pallas as pl
from jax.experimental.pallas import tpu as pltpu
from jax.sharding import PartitionSpec as P

PAD = 16
ADAM_STEP = 3
MESH = pl.DeviceIdType.MESH
NX, NY, NZ = 4, 8, 16
REACH = NZ // 2
NEAR_FIRST = (1, 7, 6, 4, 5, 3, 2)
HOPS = {0: (2, 1), 2: (2, 1), 4: (2, 1), 6: (2, 1)}
ORDER = (2, 1, 4, 3, 6, 5, 8, 7)
HIGHEST = lax.Precision.HIGHEST
F32 = jnp.float32
BF16 = jnp.bfloat16


def iota(shape, dim):
    return lax.broadcasted_iota(jnp.int32, shape, dim)


def kernel(
    grads, routes_in, gates_in, hidden, first_prev, second_prev,
    ratio, lr_out,
    tok, info, info_y, info_own, grads_here, hid, hid_pass, hid_t, sent, part, send_x, recv_x, own, relay, vec, norms, mom1, mom2,
    routes, gates,
    sem_local, sem_tok, sem_send_tok, sem_info, sem_send_info,
    sem_z, sem_z_info, sem_send_z, sem_send_zi, sem_sib, sem_sib_info, sem_send_sib, sem_send_sibi,
    sem_hand, sem_send_hand, sem_h, sem_send_h, sem_sib_h, sem_send_sib_h,
    sem_x, sem_send_x, sem_relay, sem_send_relay, sem_vec, sem_send_vec, sem_norms, sem_send_norms,
):
    expert = lax.axis_index("expert")
    dp = lax.axis_index("dp")
    z, core = expert // 2, expert % 2
    y, x = dp // NX, dp % NX
    tokens = routes_in.shape[2]
    width = grads.shape[2] // NY
    slots, units = hidden.shape[2], hidden.shape[3]
    owned = units // (NX * NY)
    cap = slots // (2 * NZ)
    sources = 2 * NZ
    all_tokens = sources * tokens
    quarter = NY * tokens // 2
    half = slots // 2

    def at_x(k):
        return {"dp": y * NX + k}

    def at_y(k):
        return {"dp": k * NX + x}

    def at_z(k):
        return {"expert": k * 2 + core}

    def core1_at_y(k):
        return {"expert": z * 2 + 1, "dp": k * NX + x}

    sibling = {"expert": z * 2 + 1 - core}

    def remote(src, dst, send, recv, where):
        return pltpu.make_async_remote_copy(
            src_ref=src, dst_ref=dst, send_sem=send, recv_sem=recv, device_id=where, device_id_type=MESH
        )

    def arrived(ref, sem):
        remote(ref, ref, sem_send_hand, sem, sibling).wait_recv()

    def left(ref, sem):
        remote(ref, ref, sem, sem_hand, sibling).wait_send()

    def columns(k):
        return pl.ds(pl.multiple_of(k * width, width), width)

    def rows(k, count):
        return pl.ds(pl.multiple_of(k * count, count), count)

    local = [
        pltpu.make_async_copy(routes_in, routes, sem_local.at[0]),
        pltpu.make_async_copy(gates_in, gates, sem_local.at[1]),
        pltpu.make_async_copy(hidden.at[0, 0], hid.at[y], sem_local.at[2]),
        pltpu.make_async_copy(first_prev.at[0], mom1, sem_local.at[3]),
        pltpu.make_async_copy(second_prev.at[0], mom2, sem_local.at[4]),
        pltpu.make_async_copy(grads.at[0], grads_here, sem_local.at[5]),
    ]
    for copy in local:
        copy.start()

    barrier = pltpu.get_barrier_semaphore()

    def greet(where):
        pl.semaphore_signal(barrier, inc=1, device_id=where, device_id_type=MESH)

    greet(sibling)
    for k in range(1, NY):
        greet({"expert": z * 2 + 1 - core, "dp": ((y + k) % NY) * NX + x})
    for k in range(1, NX * NY):
        greet({"dp": (dp + k) % (NX * NY)})

    @pl.when(core == 1)
    def _():
        for k in (1, 2, NZ - 2, NZ - 1):
            greet(at_z((z + k) % NZ))

    lane_of = iota((tokens, 128), 1) % tokens == iota((tokens, 128), 0)
    spread_out = jnp.where(lane_of, 1.0, 0.0)
    choice = iota((8, 128), 0) == iota((8, 128), 1) // tokens
    local[0].wait()
    local[1].wait()
    wide = jnp.dot(routes[0].astype(F32), spread_out, preferred_element_type=F32)
    info_own[0:1] = jnp.sum(jnp.where(choice, wide, 0.0), axis=0, keepdims=True)
    wide = jnp.dot(gates[0], spread_out, preferred_element_type=F32, precision=HIGHEST)
    info_own[1:2] = jnp.sum(jnp.where(choice, wide, 0.0), axis=0, keepdims=True)

    @pl.when(core == 1)
    def _():
        pl.semaphore_wait(barrier, NX * NY - 1 + NY + 4)

    @pl.when(core == 0)
    def _():
        pl.semaphore_wait(barrier, NX * NY - 1 + NY)

    local[5].wait()

    def token_send(k, where):
        place = (1 - k) % NY
        remote(
            grads_here.at[:, columns((y + k) % NY)], tok.at[expert, pl.ds(place * tokens, tokens)], sem_send_tok,
            sem_tok.at[core, 2 * place // NY], where,
        ).start()

    @pl.when(core == 0)
    def _():
        token_send(0, sibling)

    for k in NEAR_FIRST:
        token_send(k, core1_at_y((y + k) % NY))

    @pl.when(core == 1)
    def _():
        pltpu.make_async_copy(grads_here.at[:, columns(y)], tok.at[expert, pl.ds(tokens, tokens)], sem_tok.at[core, 0]).start()
        remote(hidden.at[0, 0], hid_pass.at[y], sem_send_hand, sem_hand, sibling).start()

    up, down = at_y((y + 1) % NY), at_y((y + NY - 1) % NY)

    def hid_copy(e, r, h, where, first=False):
        held = hid_pass if e else hid
        ref = held.at[r, pl.ds(half * h, half)]
        src = hidden.at[0, 0, pl.ds(half * h, half)] if first and not e else ref
        return remote(src, ref, sem_send_h.at[e], sem_h.at[r, e, h], where)

    @pl.when(core == 0)
    def _():
        for h in range(2):
            hid_copy(0, y, h, up, True).start()
            hid_copy(0, y, h, down, True).start()

    for k in NEAR_FIRST:
        remote(
            info_own, info_y.at[core * NY + (1 - k) % NY], sem_send_info, sem_info, core1_at_y((y + k) % NY)
        ).start()

    @pl.when(core == 0)
    def _():
        remote(info_own, info_y.at[core * NY + 1], sem_send_info, sem_info, sibling).start()

        def hand_over(r, h):
            ref = hid_pass.at[r, pl.ds(half * h, half)]
            remote(ref, hid.at[r, pl.ds(half * h, half)], sem_send_sib_h, sem_sib_h, sibling).start()

        arrived(hid_pass.at[y], sem_hand)
        for h in range(2):
            hid_copy(1, y, h, up).start()
            hid_copy(1, y, h, down).start()
        for d in range(1, 5):
            below, above = (y + NY - d) % NY, (y + d) % NY
            for e in range(2):
                for h in range(2):
                    if d < 4 or e == 0:
                        hid_copy(e, below, h, up).wait_recv()
                        if d < 3 or (d == 3 and e == 0):
                            hid_copy(e, below, h, up).start()
                        if e == 1:
                            hand_over(below, h)
                    if d < 4 or e == 1:
                        hid_copy(e, above, h, down).wait_recv()
                        if d < 3 or (d == 3 and e == 1):
                            hid_copy(e, above, h, down).start()
                        if e == 1:
                            hand_over(above, h)
        local[2].wait()

    subs = ((0, 0), (1, 0), (0, 1), (1, 1))

    @pl.when(core == 1)
    def _():
        right = [at_z((z + k) % NZ) for k in (1, 2)]
        left_ = [at_z((z + NZ - k) % NZ) for k in (1, 2)]

        def tok_ref(zz, c, h):
            return tok.at[2 * zz + c, pl.ds(quarter * h, quarter)]

        def tok_copy(zz, c, h, where):
            ref = tok_ref(zz, c, h)
            return remote(ref, ref, sem_send_z, sem_z.at[zz, 2 * c + h], where)

        def tok_share(zz, c, h):
            ref = tok_ref(zz, c, h)
            remote(ref, ref, sem_send_sib, sem_sib, sibling).start()

        def info_ref(zz):
            return info.at[pl.ds(pl.multiple_of(2 * zz, 2), 2)]

        def info_copy(zz, where):
            return remote(info_ref(zz), info_ref(zz), sem_send_zi, sem_z_info.at[zz], where)

        def info_share(zz):
            remote(info_ref(zz), info_ref(zz), sem_send_sibi, sem_sib_info, sibling).start()

        def tok_send(zz, c, h, where):
            for there in where:
                tok_copy(zz, c, h, there).start()

        def info_send(zz, where):
            for there in where:
                info_copy(zz, there).start()

        for c, h in subs:
            arrived(tok_ref(z, c, h), sem_tok.at[c, h])
            tok_send(z, c, h, [way[k - 1] for k in HOPS[0] for way in (right, left_)])
            tok_share(z, c, h)
        info_y[core * NY + 1] = info_own[...]
        arrived(info_y.at[pl.ds(0, 2 * NY - 1)], sem_info)
        for c in range(2):
            both_rows = [info_y[NY * c : NY * (c + 1), i, :] for i in range(2)]
            info[2 * z + c] = jnp.concatenate(both_rows, axis=0).astype(BF16)
        info_send(z, [way[k - 1] for k in HOPS[0] for way in (right, left_)])
        info_share(z)

        def receive(d):
            on = HOPS.get(d, ())
            from_left, from_right = (z + NZ - d) % NZ, (z + d) % NZ
            ways = ((from_left, right, 1), (from_right, left_, 0))
            for c, h in subs:
                for source, where, far_core in ways:
                    if d < REACH or c == far_core:
                        tok_copy(source, c, h, where[0]).wait_recv()
                        tok_send(source, c, h, [where[k - 1] for k in on if d + k < REACH or c == far_core])
                        tok_share(source, c, h)
            for source, where, far_core in ways:
                if d < REACH or far_core == 1:
                    info_copy(source, where[0]).wait_recv()
                    info_send(source, [where[k - 1] for k in on if d + k < REACH or far_core == 1])
                    info_share(source)

        for d in ORDER:
            receive(d)
        local[2].wait()
        arrived(hid.at[pl.ds(0, NY - 1)], sem_sib_h)

    def hid_at(place):
        return (y + NY - 1 + place) % NY

    for k in range(NY * slots // 128):
        first, last = 128 * k // slots, (128 * k + 127) // slots
        begin = 128 * k - first * slots
        if first == last:
            piece = hid[hid_at(first), begin : begin + 128, :]
        else:
            cut = slots - begin
            piece = jnp.concatenate([hid[hid_at(first), begin:slots, :], hid[hid_at(last), 0 : 128 - cut, :]], axis=0)
        piece = piece.astype(F32).T.reshape(NY, NX, owned, 128)
        for i in range(NX):
            hid_t[i, :, 128 * k : 128 * (k + 1)] = piece[:, i].reshape(NY * owned, 128).astype(BF16)

    @pl.when(core == 0)
    def _():
        arrived(info, sem_sib_info)

    pairs = sources * NY
    both = info[...].astype(F32)
    hit = both[:, 0:NY, :].reshape(pairs, 128) == expert.astype(F32)
    fold = jnp.where(iota((128, 128), 0) % tokens == iota((128, 128), 1), 1.0, 0.0)
    named = jnp.dot(jnp.where(hit, 1.0, 0.0).astype(BF16), fold.astype(BF16), preferred_element_type=F32)
    gate = jnp.dot(
        jnp.where(hit, both[:, NY : 2 * NY, :].reshape(pairs, 128), 0.0), fold, preferred_element_type=F32,
        precision=HIGHEST,
    )
    before = jnp.where(iota((128, 128), 0) < iota((128, 128), 1), 1.0, 0.0).astype(BF16)
    place = jnp.dot(named.astype(BF16), before, preferred_element_type=F32)
    target = jnp.where(named > 0.5, place + (cap * (iota(named.shape, 0) // NY)).astype(F32), -1.0)
    by_replica = jnp.sum(named.reshape(sources, NY, 128), axis=0)
    routed = jnp.sum(by_replica, axis=1, keepdims=True)
    padded = jnp.floor((routed + (PAD - 1.0)) * (1.0 / PAD)) * PAD
    total = jnp.sum(padded, axis=0, keepdims=True)
    repeat = jnp.where(iota((128, all_tokens), 0) == iota((128, all_tokens), 1) % tokens, 1.0, 0.0)
    target = jnp.dot(target.astype(BF16), repeat.astype(BF16), preferred_element_type=F32)
    gate = jnp.dot(gate, repeat, preferred_element_type=F32, precision=HIGHEST)
    own_row = iota((sources, NY, all_tokens), 0) == iota((sources, NY, all_tokens), 2) // tokens
    target = jnp.sum(jnp.where(own_row, target.reshape(own_row.shape), 0.0), axis=0)
    gate = jnp.sum(jnp.where(own_row, gate.reshape(own_row.shape), 0.0), axis=0)
    slot_id = iota((slots, all_tokens), 0).astype(F32)

    @pl.when(core == 0)
    def _():
        arrived(tok, sem_sib)

    for r in range(NY):
        target_r, gate_r = target[r : r + 1], gate[r : r + 1]
        chosen = slot_id == target_r
        gate_col = jnp.sum(jnp.where(chosen, gate_r, 0.0), axis=1, keepdims=True)
        block = tok[:, tokens * r : tokens * (r + 1), :].reshape(all_tokens, width)
        picked = jnp.dot(jnp.where(chosen, 1.0, 0.0).astype(BF16), block, preferred_element_type=F32)
        sent[slots * r : slots * (r + 1), :] = (picked * gate_col).astype(BF16)

    def x_send(k, rows_of):
        peer = (x + k) % NX
        send_x[peer] = rows_of.astype(BF16)
        remote(send_x.at[peer], recv_x.at[x], sem_send_x.at[k], sem_x.at[x], at_x(peer)).start()

    for pair in ((2, 1), (3, 0)):
        hid_rows = jnp.concatenate([hid_t[(x + k) % NX] for k in pair], axis=0)
        product = jnp.dot(hid_rows, sent[...], preferred_element_type=F32)
        for i, k in enumerate(pair):
            rows_of = product[NY * owned * i : NY * owned * (i + 1)]
            if k:
                x_send(k, rows_of)
            else:
                part[...] = rows_of

    over = (((1,), (1,)), ((), ()))
    spread = jnp.zeros((1, 1), F32)
    for r in range(NY):
        sent_r = sent[slots * r : slots * (r + 1), :]
        hid_r = hid[hid_at(r)]
        gram_h = lax.dot_general(hid_r, hid_r, over, preferred_element_type=F32)
        gram_s = lax.dot_general(sent_r, sent_r, over, preferred_element_type=F32)
        both_grams = jnp.sum(gram_h * gram_s, axis=0, keepdims=True)
        spread = spread + jnp.sum(both_grams, axis=1, keepdims=True)

    sub = iota((2, 128), 0)
    vec[dp] = jnp.where(sub == 0, spread, total * (1.0 / NY))

    def to_all(ref, send, recv):
        for k in (4, 3, 5, 2, 6, 1, 7):
            for i in range(NX):
                peer = ((y + k) % NY) * NX + (x + i) % NX
                remote(ref, ref, send, recv, {"dp": peer}).start()
        for i in range(1, NX):
            remote(ref, ref, send, recv, at_x((x + i) % NX)).start()

    to_all(vec.at[dp], sem_send_vec, sem_vec)

    summed = part[...]
    for k in (1, 3, 2):
        peer = (x + k) % NX
        arrived(recv_x.at[peer], sem_x.at[peer])
        summed = summed + recv_x[peer].astype(F32)

    power = jnp.sum(jnp.sum(summed * summed, axis=0, keepdims=True), axis=1, keepdims=True)
    norms[dp] = jnp.broadcast_to(power, (1, 128))
    to_all(norms.at[dp], sem_send_norms, sem_norms)
    for k in range(NY):
        piece = summed[owned * k : owned * (k + 1), :]
        own[k] = jnp.concatenate([piece[:, : width // 2], piece[:, width // 2 :]], axis=0).astype(BF16)
    for k in (4, 3, 5, 2, 6, 1, 7):
        peer = (y + k) % NY
        remote(own.at[peer], relay.at[y], sem_send_relay, sem_relay, at_y(peer)).start()
    relay[y] = own[y]
    local[3].wait()
    local[4].wait()
    arrived(vec.at[pl.ds(0, NX * NY - 1)], sem_vec)
    scalars = vec[0]
    for k in range(1, NX * NY):
        scalars = scalars + vec[k]
    spread, total = scalars[0:1, 0:1], scalars[1:2, 0:1]
    arrived(relay.at[pl.ds(0, NY - 1)], sem_relay)
    for k in range(NY):
        rows_k = relay[k].astype(F32)
        for h in range(2):
            cols = pl.ds(width * k + width // 2 * h, width // 2)
            mean = rows_k[owned * h : owned * (h + 1)] / total
            first = 0.9 * mom1[:, cols] + 0.1 * mean
            second = 0.95 * mom2[:, cols] + 0.05 * mean * mean
            mom1[:, cols] = (first / (1.0 - 0.9**ADAM_STEP)) / (
                jnp.sqrt(second / (1.0 - 0.95**ADAM_STEP)) + 1e-08
            )
    write = pltpu.make_async_copy(mom1, ratio.at[0], sem_local.at[0])
    write.start()
    arrived(norms.at[pl.ds(0, NX * NY - 1)], sem_norms)
    power = norms[0]
    for k in range(1, NX * NY):
        power = power + norms[k]
    power = power[:, 0:1]
    replicas = float(NX * NY)
    noise = total * spread / (replicas * power + 1e-06)
    lr_scale = noise / (noise + total / replicas)
    lr_out[0] = lr_scale[0, 0]

    write.wait()
    tok_flat = tok.at[0, pl.ds(0, tokens * (NY - 1))]
    left(tok_flat, sem_send_tok)
    left(info_y.at[pl.ds(0, NY - 1)], sem_send_info)
    for k in (2, 1, 3):
        left(send_x.at[(x + k) % NX], sem_send_x.at[k])
    left(relay.at[pl.ds(0, NY - 1)], sem_send_relay)
    left(vec.at[pl.ds(0, NX * NY - 1)], sem_send_vec)
    left(norms.at[pl.ds(0, NX * NY - 1)], sem_send_norms)

    @pl.when(core == 0)
    def _():
        left(tok.at[0, pl.ds(0, tokens)], sem_send_tok)
        left(info_y.at[0], sem_send_info)
        for e in range(2):
            left(hid.at[pl.ds(0, NY - 1)], sem_send_h.at[e])
        left(hid.at[pl.ds(0, NY - 1)], sem_send_sib_h)

    @pl.when(core == 1)
    def _():
        left(hid.at[0], sem_send_hand)
        left(tok.at[pl.ds(0, 30)], sem_send_z)
        left(tok, sem_send_sib)
        left(info.at[pl.ds(0, 30)], sem_send_zi)
        left(info, sem_send_sibi)


def on_device(out_grad, routes, gate_probs, hidden, first_prev, second_prev):
    routes = jnp.swapaxes(routes, 1, 2)
    gate_probs = jnp.swapaxes(gate_probs, 1, 2)
    tokens, width = out_grad.shape[1], out_grad.shape[2] // NY
    slots, units = hidden.shape[2:]
    owned = units // (NX * NY)
    dma = pltpu.SemaphoreType.DMA
    hbm = pl.BlockSpec(memory_space=pltpu.HBM)
    ratio, lr_scale = pl.pallas_call(
        kernel,
        out_shape=(
            jax.ShapeDtypeStruct(first_prev.shape, F32),
            jax.ShapeDtypeStruct((1,), F32),
        ),
        in_specs=[hbm] * 6,
        out_specs=(hbm, pl.BlockSpec(memory_space=pltpu.SMEM)),
        scratch_shapes=[
            pltpu.VMEM((2 * NZ, NY * tokens, width), BF16),
            pltpu.VMEM((2 * NZ, 2 * NY, 128), BF16),
            pltpu.VMEM((2 * NY, 2, 128), F32),
            pltpu.VMEM((2, 128), F32),
            pltpu.VMEM(out_grad.shape[1:], BF16),
            pltpu.VMEM((NY, slots, units), BF16),
            pltpu.VMEM((NY, slots, units), BF16),
            pltpu.VMEM((NX, NY * owned, NY * slots), BF16),
            pltpu.VMEM((NY * slots, width), BF16),
            pltpu.VMEM((NY * owned, width), F32),
            pltpu.VMEM((NX, NY * owned, width), BF16),
            pltpu.VMEM((NX, NY * owned, width), BF16),
            pltpu.VMEM((NY, 2 * owned, width // 2), BF16),
            pltpu.VMEM((NY, 2 * owned, width // 2), BF16),
            pltpu.VMEM((NX * NY, 2, 128), F32),
            pltpu.VMEM((NX * NY, 1, 128), F32),
            pltpu.VMEM(first_prev.shape[1:], F32),
            pltpu.VMEM(first_prev.shape[1:], F32),
            pltpu.VMEM(routes.shape, jnp.int32),
            pltpu.VMEM(routes.shape, F32),
            dma((6,)),
            dma((2, 2)),
            dma,
            dma,
            dma,
            dma((NZ, 4)),
            dma((NZ,)),
            dma,
            dma,
            dma,
            dma,
            dma,
            dma,
            dma,
            dma,
            dma((NY, 2, 2)),
            dma((2,)),
            dma,
            dma,
            dma((NX,)),
            dma((NX,)),
            dma,
            dma,
            dma,
            dma,
            dma,
            dma,
        ],
        compiler_params=pltpu.CompilerParams(
            collective_id=0, has_side_effects=True, vmem_limit_bytes=60 * 1024 * 1024
        ),
    )(out_grad, routes, gate_probs, hidden, first_prev, second_prev)
    return -lr_scale[0] * ratio, lr_scale


def solution(mesh):
    return jax.shard_map(
        on_device,
        mesh=mesh,
        in_specs=(
            P("dp", "expert", None),
            P("dp", "expert", None),
            P("dp", "expert", None),
            P("dp", "expert", None, None),
            P("expert", "dp", None),
            P("expert", "dp", None),
        ),
        out_specs=(P("expert", "dp", None), P("expert")),
        check_vma=False,
    )
```
